256 devices in a mesh: pts: 16 (over z_hi, x, core), cen: 16 (over y, z_lo).
Axes of the slice: x: 4, y: 4, z: 8 (z_hi: 2, z_lo: 4; z = z_hi * 4 + z_lo), core: 2. Of those that a mesh axis runs over, the one named last changes fastest.
Arguments:
- sample_vectors: float32 [12288, 1024], P('pts'), may hold values from -4 to 4
- centroids: float32 [1024, 16384], P(None, 'cen'), may hold values from -1 to 1
Outputs:
- responsibilities: float32 [12288, 16384], P('pts', 'cen')
- new_centroids: float32 [1024, 16384], P('pts', 'cen')
The draws below stay inside these ranges and needn't reach their ends.
All inputs are finite; a program needn't handle non-finite values.
Results may differ from the reference program's by a relative error of at most 0.00075.
Values sent between devices are 32-bit elements; how exact they have to be, the bound alone decides.
No kernel may reach another device: no remote copies, remote signals or barrier semaphores. Data moves between devices by JAX's collectives and lax.ppermute only.
A program may use at most 128 MiB of HBM per device.

```python
import jax
import jax.numpy as jnp
from jax import lax

D = 1024
CENTROIDS = 16384
POINTS = 12288


def centroid_base(key):
    base_key = jax.random.fold_in(key, 11)
    return 0.1 * jnp.clip(jax.random.normal(base_key, (D, CENTROIDS), jnp.float32), -5.0, 5.0)


def draw_centroids(key, part):
    base = centroid_base(key)
    return base


def draw_sample_vectors(key, part):
    key = jax.random.fold_in(key, 3)
    return 0.1 * jnp.clip(jax.random.normal(key, (POINTS, D), jnp.float32), -4.0, 4.0)


def setup_inputs(seed: int = 0) -> dict:
    key_of = jax.random.split(jax.random.key(seed), 3)
    return {
        "sample_vectors": draw_sample_vectors(jax.random.fold_in(key_of[2], 71), 0),
        "centroids": draw_centroids(jax.random.fold_in(key_of[2], 71), 0),
    }


smoothing_divisor = 0.1
prior_weight = 1.0


def soft_weights(sample_vectors, resident_prototypes):
    prototype_sq_length = jnp.sum(resident_prototypes * resident_prototypes, axis=0)
    membership_affinity = (jnp.dot(sample_vectors, resident_prototypes, precision=lax.Precision.HIGHEST, preferred_element_type=jnp.float32) - 0.5 * prototype_sq_length) / smoothing_divisor
    top = jnp.max(membership_affinity, axis=1, keepdims=True)
    expo = jnp.exp(membership_affinity - top)
    return expo / jnp.sum(expo, axis=1, keepdims=True)


def reference(sample_vectors, centroids):
    resident_prototypes = centroids
    weights = None
    for step in range(2):
        weights = soft_weights(sample_vectors, resident_prototypes)
        cluster_mass = jnp.sum(weights, axis=0)
        moments = lax.dot_general(sample_vectors, weights, (((0,), (0,)), ((), ())), precision=lax.Precision.HIGHEST, preferred_element_type=jnp.float32)
        resident_prototypes = (moments + prior_weight * resident_prototypes) / (cluster_mass + prior_weight)
    return weights, resident_prototypes
```

```python
import functools

import jax
import jax.numpy as jnp
from jax import lax
from jax.experimental import pallas as pl
from jax.experimental.pallas import tpu as pltpu
from jax.sharding import PartitionSpec as P

F32 = jnp.float32
BF16 = jnp.bfloat16
PAD = 8
MIB = 1 << 20
CORE, XA, XB, ZG = 1, 2, 6, 8
UNITS = ((0.5, (CORE, XA, XB, ZG)), (0.5, (CORE, XB, XA, ZG)))


def split(v):
    hi = v.astype(BF16)
    return hi, (v - hi.astype(F32)).astype(BF16)


def dot3(ah, al, bh, bl):
    dot = functools.partial(jnp.dot, preferred_element_type=F32)
    return dot(ah, bh) + (dot(ah, bl) + dot(al, bh))


def relative_blocks(gens):
    out = [0]
    for g in reversed(gens):
        out = out + [r ^ g for r in out]
    return out


def swap(v, g):
    return lax.ppermute(v, "pts", [(i, i ^ g) for i in range(lax.axis_size("pts"))])


def params(mib):
    return pltpu.CompilerParams(vmem_limit_bytes=mib * MIB)


def cost(flops, nbytes):
    return pl.CostEstimate(flops=int(flops), bytes_accessed=int(nbytes), transcendentals=0)


def softmax_part(raw, half_norm, e_ref, stat_ref):
    logits = (raw - half_norm) * 10.0
    top = jnp.max(logits, axis=1, keepdims=True)
    expo = jnp.exp(logits - top)
    total = jnp.sum(expo, axis=1, keepdims=True)
    e_ref[...] = expo
    rows = raw.shape[0]
    stat_ref[0:1, :] = jnp.broadcast_to(top, (rows, 128)).T[0:1, :]
    stat_ref[1:2, :] = jnp.broadcast_to(total, (rows, 128)).T[0:1, :]


def first_kernel(x_ref, c_ref, e_ref, stat_ref, xh_ref, xl_ref, th_ref, tl_ref, ch, cl, norm):
    @pl.when(pl.program_id(0) == 0)
    def _():
        c = c_ref[...]
        ch[...], cl[...] = split(c)
        norm[0:1, :] = 0.5 * jnp.sum(c * c, axis=0, keepdims=True)

    x = x_ref[...]
    xh, xl = split(x)
    xh_ref[...] = xh
    xl_ref[...] = xl
    th_ref[...], tl_ref[...] = split(x.T)
    softmax_part(dot3(xh, xl, ch[...], cl[...]), norm[0:1, :], e_ref, stat_ref)


def first_step(x, c, tile=256):
    n, d = x.shape
    k = c.shape[1]
    return pl.pallas_call(
        first_kernel,
        grid=(n // tile,),
        in_specs=[
            pl.BlockSpec((tile, d), lambda i: (i, 0)),
            pl.BlockSpec((d, k), lambda i: (0, 0)),
        ],
        out_specs=[
            pl.BlockSpec((tile, k), lambda i: (i, 0)),
            pl.BlockSpec((2, tile), lambda i: (0, i)),
            pl.BlockSpec((tile, d), lambda i: (i, 0)),
            pl.BlockSpec((tile, d), lambda i: (i, 0)),
            pl.BlockSpec((d, tile), lambda i: (0, i)),
            pl.BlockSpec((d, tile), lambda i: (0, i)),
        ],
        out_shape=[
            jax.ShapeDtypeStruct((n, k), F32),
            jax.ShapeDtypeStruct((2, n), F32),
            jax.ShapeDtypeStruct((n, d), BF16),
            jax.ShapeDtypeStruct((n, d), BF16),
            jax.ShapeDtypeStruct((d, n), BF16),
            jax.ShapeDtypeStruct((d, n), BF16),
        ],
        scratch_shapes=[
            pltpu.VMEM((d, k), BF16),
            pltpu.VMEM((d, k), BF16),
            pltpu.VMEM((8, k), F32),
        ],
        compiler_params=params(48),
        cost_estimate=cost(6 * n * d * k, 4 * (2 * n * d + d * k + n * k)),
        name="first_logits",
    )(x, c)


def next_kernel(layout, me_ref, *refs):
    n_in = 2 * len(layout)
    pieces = refs[:n_in]
    xh_ref, xl_ref, e_ref, stat_ref, ch, cl, norm = refs[n_in:]

    @pl.when(pl.program_id(0) == 0)
    def _():
        me = me_ref[0]
        for u, (start, width, order) in enumerate(layout):
            cols = slice(start, start + width)
            half = len(order) // 2
            rows = pieces[2 * u].shape[0] // half
            total = jnp.zeros((1, width), F32)
            for j, r in enumerate(order):
                piece = pieces[2 * u + j // half]
                v = piece[(j % half) * rows : (j % half + 1) * rows, :]
                hi, lo = split(v)
                at = pl.ds(pl.multiple_of((me ^ r) * rows, rows), rows)
                ch[at, cols] = hi
                cl[at, cols] = lo
                total = total + jnp.sum(v * v, axis=0, keepdims=True)
            norm[0:1, cols] = 0.5 * total

    softmax_part(
        dot3(xh_ref[...], xl_ref[...], ch[...], cl[...]), norm[0:1, :], e_ref, stat_ref
    )


def next_step(me, pieces, layout, xh, xl, tile=256):
    n, d = xh.shape
    k = sum(width for _, width, _ in layout)
    flat = [p for pair in pieces for p in pair]
    return pl.pallas_call(
        functools.partial(next_kernel, layout),
        grid=(n // tile,),
        in_specs=[pl.BlockSpec(memory_space=pltpu.SMEM)]
        + [pl.BlockSpec(p.shape, lambda i: (0, 0)) for p in flat]
        + [pl.BlockSpec((tile, d), lambda i: (i, 0))] * 2,
        out_specs=[
            pl.BlockSpec((tile, k), lambda i: (i, 0)),
            pl.BlockSpec((2, tile), lambda i: (0, i)),
        ],
        out_shape=[
            jax.ShapeDtypeStruct((n, k), F32),
            jax.ShapeDtypeStruct((2, n), F32),
        ],
        scratch_shapes=[
            pltpu.VMEM((d, k), BF16),
            pltpu.VMEM((d, k), BF16),
            pltpu.VMEM((8, k), F32),
        ],
        compiler_params=params(48),
        cost_estimate=cost(6 * n * d * k, 4 * (n * d + d * k + n * k)),
        name="next_logits",
    )(me, *flat, xh, xl)


def row_scale(own, everyone):
    tops = everyone[:, 0, :]
    top = jnp.max(tops, axis=0, keepdims=True)
    total = jnp.sum(everyone[:, 1, :] * jnp.exp(tops - top), axis=0, keepdims=True)
    return jnp.exp(own[0:1, :] - top) / total


def moment_kernel(order, me_ref, own_ref, all_ref, th_ref, tl_ref, e_ref, keep_ref, send_ref, ph, pt):
    me = me_ref[0]
    rows = th_ref.shape[0] // len(order)
    for j, r in enumerate(order):
        at = pl.ds(pl.multiple_of((me ^ r) * rows, rows), rows)
        ph[j * rows : (j + 1) * rows, :] = th_ref[at, :]
        pt[j * rows : (j + 1) * rows, :] = tl_ref[at, :]
    scale = row_scale(own_ref[...], all_ref[...])
    n = scale.shape[1]
    column = jnp.broadcast_to(scale, (128, n)).T[:, 0:1]
    w = e_ref[...] * column
    wh, wl = split(w)
    m = dot3(ph[...], pt[...], wh, wl)
    half = m.shape[0] // 2
    mass = jnp.broadcast_to(jnp.sum(w, axis=0, keepdims=True), (PAD, w.shape[1]))
    keep_ref[0:half, :] = m[:half]
    send_ref[0:half, :] = m[half:]
    keep_ref[half : half + PAD, :] = mass
    send_ref[half : half + PAD, :] = mass


def moment_step(me, own, everyone, th, tl, e, start, width, order):
    d, n = th.shape
    shape = jax.ShapeDtypeStruct((d // 2 + PAD, width), F32)
    whole = lambda a: pl.BlockSpec(a.shape, lambda i: (0,) * a.ndim)
    col = start // width
    return pl.pallas_call(
        functools.partial(moment_kernel, order),
        grid=(1,),
        in_specs=[
            pl.BlockSpec(memory_space=pltpu.SMEM),
            whole(own),
            whole(everyone),
            whole(th),
            whole(tl),
            pl.BlockSpec((n, width), lambda i: (0, col)),
        ],
        out_specs=[whole(shape), whole(shape)],
        out_shape=[shape, shape],
        scratch_shapes=[pltpu.VMEM((d, n), BF16), pltpu.VMEM((d, n), BF16)],
        compiler_params=params(48),
        cost_estimate=cost(6 * d * n * width, 4 * (d * n + n * width + d * width)),
        name="moments",
    )(me, own, everyone, th, tl, e)


def fold_kernel(keep_ref, recv_ref, out_ref, send_ref):
    half = (keep_ref.shape[0] - PAD) // 2
    out_ref[0:half, :] = keep_ref[0:half, :] + recv_ref[0:half, :]
    send_ref[0:half, :] = keep_ref[half : 2 * half, :] + recv_ref[half : 2 * half, :]
    mass = keep_ref[2 * half :, :] + recv_ref[2 * half :, :]
    out_ref[half:, :] = mass
    send_ref[half:, :] = mass


def fold(keep, recv):
    rows = (keep.shape[0] - PAD) // 2 + PAD
    shape = jax.ShapeDtypeStruct((rows, keep.shape[1]), F32)
    return pl.pallas_call(
        fold_kernel,
        out_shape=[shape, shape],
        compiler_params=params(16),
        cost_estimate=cost(keep.size, 16 * keep.size),
        name="fold",
    )(keep, recv)


def update_kernel(parts, keep_ref, recv_ref, old_ref, out_ref):
    rows = keep_ref.shape[0] - PAD
    mass = keep_ref[rows : rows + 1, :] + recv_ref[rows : rows + 1, :] + 1.0
    block = rows // parts
    for i in range(parts):
        here = slice(i * block, (i + 1) * block)
        there = slice((parts - 1 - i) * block, (parts - i) * block)
        out_ref[here, :] = (keep_ref[here, :] + recv_ref[there, :] + old_ref[here, :]) / mass


def scatter(keep, send, gens):
    for g in gens[:-1]:
        keep, send = fold(keep, swap(send, g))
    return keep, send


def old_rows(c, me, start, width, last, rows):
    parts = [
        lax.dynamic_slice(c, ((me[0] ^ r) * rows, jnp.int32(start)), (rows, width))
        for r in (0, last)
    ]
    return jnp.concatenate(parts, axis=0)


def update(keep, recv, old, parts=1):
    return pl.pallas_call(
        functools.partial(update_kernel, parts),
        out_shape=jax.ShapeDtypeStruct(old.shape, F32),
        compiler_params=params(16),
        cost_estimate=cost(4 * old.size, 16 * old.size),
        name="update",
    )(keep, recv, old)


def everyone_stats(stats):
    size = lax.axis_size("cen")
    return lax.all_to_all(jnp.broadcast_to(stats[None], (size, *stats.shape)), "cen", 0, 0)


def local(x, c):
    me = lax.axis_index("pts").astype(jnp.int32).reshape(1)
    k = c.shape[1]
    rows = c.shape[0] // lax.axis_size("pts")
    layout, start = [], 0
    for share, gens in UNITS:
        width = int(k * share)
        layout.append((start, width, gens, relative_blocks(gens)))
        start += width

    e, stats, xh, xl, th, tl = first_step(x, c)
    everyone = everyone_stats(stats)
    moments = [
        moment_step(me, stats, everyone, th, tl, e, s, w, order) for s, w, _, order in layout
    ]
    shares, pieces = [], []
    for (s, w, gens, order), (keep, send) in zip(layout, moments):
        old = old_rows(c, me, s, w, gens[-1], rows)
        for g in gens[:-2]:
            keep, send = fold(keep, swap(send, g))
        whole = join(keep, swap(send, gens[-2]))
        share = update(whole, swap(whole, gens[-1]), old, 2)
        shares.append(share)
        cur = share
        for g in gens[-2:0:-1]:
            cur = jnp.concatenate([cur, swap(cur, g)], axis=0)
        pieces.append((cur, swap(cur, gens[0])))

    plan = [(s, w, order) for s, w, _, order in layout]
    e, stats = next_step(me, pieces, plan, xh, xl)
    everyone = everyone_stats(stats)
    outs = []
    for (s, w, gens, order), share in zip(layout, shares):
        keep, send = moment_step(me, stats, everyone, th, tl, e, s, w, order)
        keep, send = scatter(keep, send, gens)
        outs.append(update(keep, swap(send, gens[-1]), share[:rows]))
    weights = e * row_scale(stats, everyone).reshape(-1, 1)
    return weights, jnp.concatenate(outs, axis=1)


def join_kernel(keep_ref, recv_ref, out_ref):
    out_ref[...] = keep_ref[...] + recv_ref[...]


def join(keep, recv):
    return pl.pallas_call(
        join_kernel,
        out_shape=jax.ShapeDtypeStruct(keep.shape, F32),
        compiler_params=params(16),
        cost_estimate=cost(keep.size, 12 * keep.size),
        name="join",
    )(keep, recv)


def solution(mesh):
    placed = (P("pts", None), P(None, "cen"))
    return jax.shard_map(
        local,
        mesh=mesh,
        in_specs=placed,
        out_specs=(P("pts", "cen"), P("pts", "cen")),
        check_vma=False,
    )
```

```python
import functools

import jax
import jax.numpy as jnp
from jax import lax
from jax.experimental import pallas as pl
from jax.experimental.pallas import tpu as pltpu
from jax.sharding import PartitionSpec as P

F32 = jnp.float32
BF16 = jnp.bfloat16
PAD = 8
MIB = 1 << 20
CORE, XA, XB, ZG = 1, 2, 6, 8
COST = 0.1
COLORS = ((CORE, XA, XB), (CORE, XB, XA))


def split(v):
    hi = v.astype(BF16)
    return hi, (v - hi.astype(F32)).astype(BF16)


def dot3(ah, al, bh, bl):
    dot = functools.partial(jnp.dot, preferred_element_type=F32)
    return dot(ah, bh) + (dot(ah, bl) + dot(al, bh))


def relative_blocks(gens):
    out = [0]
    for g in reversed(gens):
        out = out + [r ^ g for r in out]
    return out


def swap(v, g):
    return lax.ppermute(v, "pts", [(i, i ^ g) for i in range(lax.axis_size("pts"))])


def params(mib):
    return pltpu.CompilerParams(vmem_limit_bytes=mib * MIB)


def cost(flops, nbytes):
    return pl.CostEstimate(
        flops=int(flops * COST), bytes_accessed=int(nbytes * COST), transcendentals=0
    )


def far_memory(*arrays):
    out = [pltpu.with_memory_space_constraint(a, pltpu.HBM) for a in arrays]
    return out[0] if len(out) == 1 else out


def near_memory(*arrays):
    return [pltpu.with_memory_space_constraint(a, pltpu.VMEM) for a in arrays]


ANY = pl.BlockSpec(memory_space=pl.ANY)
SMALL = pl.BlockSpec(memory_space=pltpu.SMEM)
NEAR = pl.BlockSpec(memory_space=pltpu.VMEM)


def whole(a):
    return pl.BlockSpec(a.shape, lambda i, s: (0,) * len(a.shape))


def softmax_part(raw, half_norm, e_ref):
    logits = (raw - half_norm) * 10.0
    top = jnp.max(logits, axis=1, keepdims=True)
    expo = jnp.exp(logits - top)
    total = jnp.sum(expo, axis=1, keepdims=True)
    e_ref[...] = expo
    rows = raw.shape[0]
    row = lambda v: jnp.broadcast_to(v, (rows, 128)).T[0:1, :]
    return row(top), row(total)


def put_stats(stats, stat_ref, all_ref, at):
    for i, v in enumerate(stats):
        stat_ref[i : i + 1, at] = v
        all_ref[:, i : i + 1, at] = jnp.broadcast_to(v[None], (all_ref.shape[0], *v.shape))


def first_kernel(
    me_ref, at_ref, pin_ref, x_ref, c_ref, e_ref, stat_ref, all_ref, xh_ref, xl_ref, th_ref, tl_ref, ch, cl, norm
):
    @pl.when(pl.program_id(0) == 0)
    def _():
        c = c_ref[...]
        ch[...], cl[...] = split(c)
        norm[0:1, :] = 0.5 * jnp.sum(c * c, axis=0, keepdims=True)

    x = x_ref[...]
    xh, xl = split(x)
    xh_ref[...] = xh
    xl_ref[...] = xl
    th_ref[...], tl_ref[...] = split(x.T)
    stats = softmax_part(dot3(xh, xl, ch[...], cl[...]), norm[0:1, :], e_ref)
    put_stats(stats, stat_ref, all_ref, slice(None))


def first_step(me, at, pin, x, c, copies, tile=256):
    n, d = x.shape
    k = c.shape[1]
    return pl.pallas_call(
        first_kernel,
        grid=(n // tile,),
        in_specs=[
            SMALL,
            SMALL,
            ANY,
            pl.BlockSpec((tile, d), lambda i: (i, 0)),
            pl.BlockSpec((d, k), lambda i: (0, 0)),
        ],
        out_specs=[
            pl.BlockSpec((tile, k), lambda i: (i, 0)),
            pl.BlockSpec((2, tile), lambda i: (0, i)),
            pl.BlockSpec((copies, 2, tile), lambda i: (0, 0, i)),
            pl.BlockSpec((tile, d), lambda i: (i, 0)),
            pl.BlockSpec((tile, d), lambda i: (i, 0)),
            pl.BlockSpec((d, tile), lambda i: (0, i)),
            pl.BlockSpec((d, tile), lambda i: (0, i)),
        ],
        out_shape=[
            pltpu.VMEM((n, k), F32),
            jax.ShapeDtypeStruct((2, n), F32),
            jax.ShapeDtypeStruct((copies, 2, n), F32),
            pltpu.HBM((n, d), BF16),
            pltpu.HBM((n, d), BF16),
            pltpu.VMEM((d, n), BF16),
            pltpu.VMEM((d, n), BF16),
        ],
        scratch_shapes=[
            pltpu.VMEM((d, k), BF16),
            pltpu.VMEM((d, k), BF16),
            pltpu.VMEM((8, k), F32),
        ],
        compiler_params=params(36),
        cost_estimate=cost(20 * 6 * n * d * k, 4 * (2 * n * d + d * k + n * k)),
        name="first_logits",
    )(me, at, pin, *far_memory(x, c))


def far_kernel(at_ref, *refs):
    pieces, (xh_ref, xl_ref, th_ref, tl_ref) = refs[:4], refs[4:]
    width = pieces[0].shape[1]
    for shift, piece in enumerate(pieces):
        quarter = lax.rem(at_ref[3] - shift + 4, 4)
        at = pl.ds(pl.multiple_of(quarter * width, width), width)
        v = piece[...]
        xh_ref[:, at], xl_ref[:, at] = split(v)
        th_ref[at, :], tl_ref[at, :] = split(v.T)


def far_points(at, pieces):
    n, width = pieces[0].shape
    d = width * len(pieces)
    return pl.pallas_call(
        far_kernel,
        in_specs=[SMALL] + [NEAR] * len(pieces),
        out_specs=[NEAR] * 4,
        out_shape=[pltpu.VMEM(s, BF16) for s in ((n, d), (n, d), (d, n), (d, n))],
        compiler_params=params(16),
        cost_estimate=cost(4 * n * d, 12 * n * d),
        name="far_points",
    )(at, *pieces)


def slice_kernel(at_ref, pin_ref, x_ref, out_ref):
    out_ref[...] = x_ref[...]


def own_piece(x, at):
    n, size = x.shape[0], x.shape[1] // 8
    return pl.pallas_call(
        lambda at_ref, x_ref, out_ref: slice_kernel(at_ref, None, x_ref, out_ref),
        grid_spec=pltpu.PrefetchScalarGridSpec(
            num_scalar_prefetch=1,
            grid=(1,),
            in_specs=[pl.BlockSpec((n, size), lambda i, s: (0, s[0]))],
            out_specs=pl.BlockSpec((n, size), lambda i, s: (0, 0)),
        ),
        out_shape=jax.ShapeDtypeStruct((n, size), F32),
        compiler_params=params(8),
        cost_estimate=cost(1, 8 * n * size),
        name="own_piece",
    )(at, far_memory(x))


def couple_kernel(at_ref, pin_ref, mine_ref, other_ref, out_ref):
    width = mine_ref.shape[1]
    side = at_ref[0] & 1
    out_ref[:, pl.ds(pl.multiple_of(side * width, width), width)] = mine_ref[...]
    out_ref[:, pl.ds(pl.multiple_of((1 - side) * width, width), width)] = other_ref[...]


def couple(at, pin, mine, other):
    n, width = mine.shape
    return pl.pallas_call(
        couple_kernel,
        in_specs=[SMALL, ANY, NEAR, NEAR],
        out_specs=NEAR,
        out_shape=jax.ShapeDtypeStruct((n, 2 * width), F32),
        compiler_params=params(4),
        cost_estimate=cost(1, 16 * n * width),
        name="couple",
    )(at, pin, mine, other)


def old_block(c, me, rows, width, pin):
    return pl.pallas_call(
        slice_kernel,
        grid_spec=pltpu.PrefetchScalarGridSpec(
            num_scalar_prefetch=1,
            grid=(2,),
            in_specs=[
                ANY,
                pl.BlockSpec((rows, width), lambda b, s: ((s[0] & 7) + 8 * b, s[0] // 8)),
            ],
            out_specs=pl.BlockSpec((rows, width), lambda b, s: (b, 0)),
        ),
        out_shape=jax.ShapeDtypeStruct((2 * rows, width), F32),
        compiler_params=params(4),
        cost_estimate=cost(1, 16 * rows * width),
        name="old_block",
    )(me, pin, far_memory(c))


def spread(orders, me_ref, pieces, ch, cl, norm):
    low = me_ref[0] & 7
    width = pieces[0].shape[1]
    for u, order in enumerate(orders):
        cols = slice(u * width, (u + 1) * width)
        half = len(order) // 2
        rows = pieces[2 * u].shape[0] // half // 2
        total = jnp.zeros((1, width), F32)
        for j, r in enumerate(order):
            piece = pieces[2 * u + j // half]
            for b in range(2):
                start = ((j % half) * 2 + b) * rows
                v = piece[start : start + rows, :]
                hi, lo = split(v)
                at = pl.ds(pl.multiple_of(((low ^ r) + 8 * b) * rows, rows), rows)
                ch[at, cols] = hi
                cl[at, cols] = lo
                total = total + jnp.sum(v * v, axis=0, keepdims=True)
        norm[:, cols] = jnp.broadcast_to(0.5 * total, (8, width))


def own_kernel(orders, me_ref, *refs):
    pieces = refs[: 2 * len(orders)]
    xh_ref, xl_ref, e_ref, stat_ref, ch, cl, norm = refs[2 * len(orders) :]

    @pl.when(pl.program_id(0) == 0)
    def _():
        spread(orders, me_ref, pieces, ch, cl, norm)

    raw = dot3(xh_ref[...], xl_ref[...], ch[...], cl[...])
    top, total = softmax_part(raw, norm[0:1, :], e_ref)
    stat_ref[0:1, :] = top
    stat_ref[1:2, :] = total


def own_logits(me, pieces, orders, near, tile=256):
    n, d = near[0].shape
    k = sum(pair[0].shape[1] for pair in pieces)
    flat = [p for pair in pieces for p in pair]
    shapes = [pltpu.VMEM((d, k), BF16), pltpu.VMEM((d, k), BF16), pltpu.VMEM((8, k), F32)]
    return pl.pallas_call(
        functools.partial(own_kernel, orders),
        grid_spec=pltpu.PrefetchScalarGridSpec(
            num_scalar_prefetch=1,
            grid=(n // tile,),
            in_specs=[NEAR] * len(flat) + [pl.BlockSpec((tile, d), lambda i, s: (i, 0))] * 2,
            out_specs=[
                pl.BlockSpec((tile, k), lambda i, s: (i, 0)),
                pl.BlockSpec((2, tile), lambda i, s: (0, i)),
                NEAR,
                NEAR,
                NEAR,
            ],
        ),
        out_shape=[pltpu.VMEM((n, k), F32), jax.ShapeDtypeStruct((2, n), F32), *shapes],
        compiler_params=params(24),
        cost_estimate=cost(6 * n * d * k, 4 * (n * d + d * k + n * k)),
        name="own_logits",
    )(me, *flat, *far_memory(*near))


def far_logits_kernel(
    me_ref, ch, cl, norm, own_ref, xh_ref, xl_ref, e_ref, stat_ref
):
    step = pl.program_id(0)
    tile = e_ref.shape[0]
    n = own_ref.shape[1]
    z = me_ref[0] // 8
    raw = dot3(xh_ref[...], xl_ref[...], ch[...], cl[...])
    stats = softmax_part(raw, norm[0:1, :], e_ref)
    at = pl.ds(pl.multiple_of((1 - z) * n + step * tile, tile), tile)
    for i, v in enumerate(stats):
        stat_ref[i : i + 1, at] = v

    @pl.when(step == 0)
    def _():
        stat_ref[:, pl.ds(pl.multiple_of(z * n, n), n)] = own_ref[...]


def far_logits(me, ch, cl, norm, own, far, tile=256):
    n, d = far[0].shape
    k = ch.shape[1]
    return pl.pallas_call(
        far_logits_kernel,
        grid_spec=pltpu.PrefetchScalarGridSpec(
            num_scalar_prefetch=1,
            grid=(n // tile,),
            in_specs=[NEAR] * 4 + [pl.BlockSpec((tile, d), lambda i, s: (i, 0))] * 2,
            out_specs=[pl.BlockSpec((tile, k), lambda i, s: (i, 0)), NEAR],
        ),
        out_shape=[
            pltpu.VMEM((n, k), F32),
            jax.ShapeDtypeStruct((2, 2 * n), F32),
        ],
        compiler_params=params(24),
        cost_estimate=cost(6 * n * d * k, 4 * (n * d + d * k + n * k)),
        name="far_logits",
    )(me, ch, cl, norm, own, *far)


def merge_kernel(pin_ref, mine_ref, other_ref, out_ref):
    top = jnp.maximum(mine_ref[0:1, :], other_ref[0:1, :])
    total = sum(ref[1:2, :] * jnp.exp(ref[0:1, :] - top) for ref in (mine_ref, other_ref))
    for i, v in enumerate((top, total)):
        out_ref[:, i : i + 1, :] = jnp.broadcast_to(v[None], (out_ref.shape[0], *v.shape))


def merge(pin, mine, other, copies):
    return pl.pallas_call(
        merge_kernel,
        in_specs=[ANY, NEAR, NEAR],
        out_specs=NEAR,
        out_shape=jax.ShapeDtypeStruct((copies, *mine.shape), F32),
        compiler_params=params(4),
        cost_estimate=cost(copies * mine.size, 8 * copies * mine.size),
        name="merge",
    )(pin, mine, other)


def row_scale(own, everyone):
    tops = everyone[:, 0, :]
    top = jnp.max(tops, axis=0, keepdims=True)
    total = jnp.sum(everyone[:, 1, :] * jnp.exp(tops - top), axis=0, keepdims=True)
    scale = jnp.exp(own[0:1, :] - top) / total
    return jnp.broadcast_to(scale, (128, scale.shape[1])).T[:, 0:1]


def permuted(order, low, ref, out):
    rows = ref.shape[0] // (2 * len(order))
    for j, r in enumerate(order):
        for b in range(2):
            at = pl.ds(pl.multiple_of(((low ^ r) + 8 * b) * rows, rows), rows)
            out[(2 * j + b) * rows : (2 * j + b + 1) * rows, :] = ref[at, :]


def emit(m, w, keep_ref, send_ref, at):
    half = m.shape[0] // 2
    mass = jnp.broadcast_to(jnp.sum(w, axis=0, keepdims=True), (PAD, w.shape[1]))
    keep_ref[0:half, at] = m[:half]
    send_ref[0:half, at] = m[half:]
    keep_ref[half : half + PAD, at] = mass
    send_ref[half : half + PAD, at] = mass


def first_moment_kernel(
    order, color, me_ref, pin_ref, own_ref, all_ref, th_ref, tl_ref, e_ref, keep_ref, send_ref, ph, pt
):
    low, z = me_ref[0] & 7, me_ref[0] // 8
    permuted(order, low, th_ref, ph)
    permuted(order, low, tl_ref, pt)
    scale = row_scale(own_ref[...], all_ref[...])
    width = e_ref.shape[1] // 4
    for h in range(2):
        column = pl.multiple_of((2 * (z ^ h) + color) * width, width)
        w = e_ref[:, pl.ds(column, width)] * scale
        wh, wl = split(w)
        m = dot3(ph[...], pt[...], wh, wl)
        emit(m, w, keep_ref, send_ref, slice(h * width, (h + 1) * width))


def first_moments(me, pin, own, everyone, th, tl, e, color, order):
    d, n = th.shape
    width = e.shape[1] // 4
    shape = jax.ShapeDtypeStruct((d // 2 + PAD, 2 * width), F32)
    return pl.pallas_call(
        functools.partial(first_moment_kernel, order, color),
        in_specs=[SMALL, ANY] + [NEAR] * 5,
        out_specs=[NEAR, NEAR],
        out_shape=[shape, shape],
        scratch_shapes=[pltpu.VMEM((d, n), BF16), pltpu.VMEM((d, n), BF16)],
        compiler_params=params(20),
        cost_estimate=cost(12 * d * n * width, 4 * (d * n + 2 * n * width + 2 * d * width)),
        name="first_moments",
    )(me, pin, own, everyone, th, tl, e)


def next_moment_kernel(
    order, color, me_ref, pin_ref, own, everyone, oh, ol, gh, gl, e0, e1, keep_ref, send_ref, ph, pt
):
    low, z = me_ref[0] & 7, me_ref[0] // 8
    n = e0.shape[0]
    width = e0.shape[1] // 2
    m = w_all = None
    for h, (th, tl, e) in enumerate(((oh, ol, e0), (gh, gl, e1))):
        at = pl.ds(pl.multiple_of((z ^ h) * n, n), n)
        permuted(order, low, th, ph)
        permuted(order, low, tl, pt)
        w = e[:, color * width : (color + 1) * width] * row_scale(own[:, at], everyone[:, :, at])
        wh, wl = split(w)
        part = dot3(ph[...], pt[...], wh, wl)
        m, w_all = (part, w) if m is None else (m + part, w_all + w)
    emit(m, w_all, keep_ref, send_ref, slice(None))


def next_moments(me, pin, own, everyone, near, far, e_own, e_far, color, order):
    d, n = near[0].shape
    width = e_own.shape[1] // 2
    shape = jax.ShapeDtypeStruct((d // 2 + PAD, width), F32)
    return pl.pallas_call(
        functools.partial(next_moment_kernel, order, color),
        in_specs=[SMALL, ANY] + [NEAR] * 8,
        out_specs=[NEAR, NEAR],
        out_shape=[shape, shape],
        scratch_shapes=[pltpu.VMEM((d, n), BF16)] * 2,
        compiler_params=params(20),
        cost_estimate=cost(12 * d * n * width, 4 * (2 * d * n + 2 * n * width + d * width)),
        name="next_moments",
    )(me, pin, own, everyone, *near, *far, e_own, e_far)


def relay_kernel(pin_ref, in_ref, out_ref):
    pass


def relay(a, pin):
    return pl.pallas_call(
        relay_kernel,
        in_specs=[ANY, ANY],
        out_specs=ANY,
        out_shape=jax.ShapeDtypeStruct(a.shape, a.dtype),
        input_output_aliases={1: 0},
        compiler_params=params(4),
        cost_estimate=cost(1, 1),
        name="relay",
    )(pin, a)


def fold_kernel(pins, *refs):
    refs = refs[pins:]
    count = len(refs) // 4
    for u in range(count):
        keep, recv = refs[2 * u : 2 * u + 2]
        out, send = refs[2 * (count + u) : 2 * (count + u) + 2]
        half = (keep.shape[0] - PAD) // 2
        out[0:half, :] = keep[0:half, :] + recv[0:half, :]
        send[0:half, :] = keep[half : 2 * half, :] + recv[half : 2 * half, :]
        mass = keep[2 * half :, :] + recv[2 * half :, :]
        out[half:, :] = mass
        send[half:, :] = mass


def pairs(flat):
    return [(flat[2 * i], flat[2 * i + 1]) for i in range(len(flat) // 2)]


def chain(kernel, name, ins, shapes, pins=()):
    size = sum(a.size for a in ins)
    return pl.pallas_call(
        kernel,
        in_specs=[ANY] * len(pins) + [NEAR] * len(ins),
        out_shape=[jax.ShapeDtypeStruct(shape, F32) for shape in shapes],
        compiler_params=params(12),
        cost_estimate=cost(size, 8 * size),
        name=name,
    )(*pins, *ins)


def fold(ins, *pin):
    shapes = []
    for keep, _ in ins:
        shapes += [((keep.shape[0] - PAD) // 2 + PAD, keep.shape[1])] * 2
    return pairs(chain(
            functools.partial(fold_kernel, len(pin)),
            "fold",
            [a for pair in ins for a in pair],
            shapes,
            pin,
        ))


def part_kernel(pins, *refs):
    refs = refs[pins:]
    count = len(refs) // 4
    for u in range(count):
        keep, recv = refs[2 * u : 2 * u + 2]
        out, send = refs[2 * (count + u) : 2 * (count + u) + 2]
        half = keep.shape[1] // 2
        out[...] = keep[:, 0:half] + recv[:, 0:half]
        send[...] = keep[:, half:] + recv[:, half:]


def part(ins, *pin):
    shapes = []
    for keep, _ in ins:
        shapes += [(keep.shape[0], keep.shape[1] // 2)] * 2
    return pairs(
        chain(
            functools.partial(part_kernel, len(pin)),
            "part",
            [a for pair in ins for a in pair],
            shapes,
            pin,
        )
    )


def update_kernel(pins, *refs):
    refs = refs[pins:]
    count = (len(refs) - 2) // 3
    old, joint = refs[2 * count], refs[-1]
    for u in range(count):
        keep, recv = refs[2 * u : 2 * u + 2]
        rows, width = old.shape[0], keep.shape[1]
        mass = keep[rows : rows + 1, :] + recv[rows : rows + 1, :] + 1.0
        cols = slice(u * width, (u + 1) * width)
        new = (keep[0:rows, :] + recv[0:rows, :] + old[:, cols]) / mass
        refs[2 * count + 1 + u][...] = new
        joint[:, cols] = new


def update(ins, old, *pin):
    flat = [a for pair in ins for a in pair]
    shapes = [(old.shape[0], keep.shape[1]) for keep, _ in ins] + [old.shape]
    return chain(functools.partial(update_kernel, len(pin)), "update", flat + [old], shapes, pin)


def stack_kernel(pins, *refs):
    refs = refs[pins:]
    count = len(refs) // 3
    for u in range(count):
        own, other, out = refs[2 * u], refs[2 * u + 1], refs[2 * count + u]
        rows = own.shape[0]
        out[0:rows, :] = own[...]
        out[rows:, :] = other[...]


def stack(ins, *pin):
    shapes = [(2 * own.shape[0], own.shape[1]) for own, _ in ins]
    flat = [a for pair in ins for a in pair]
    return chain(functools.partial(stack_kernel, len(pin)), "stack", flat, shapes, pin)


def column_kernel(pin_ref, *refs):
    rows = refs[0].shape[0]
    for i, ref in enumerate(refs[:-1]):
        refs[-1][i * rows : (i + 1) * rows, :] = ref[...]


def column(pieces, pin):
    rows, width = pieces[0].shape
    return chain(column_kernel, "column", pieces, [(rows * len(pieces), width)], [pin])[0]


def last_kernel(me_ref, *refs):
    ins, (mine_ref, theirs_ref) = refs[:-2], refs[-2:]
    z = me_ref[0] // 8
    for u in range(len(ins) // 3):
        keep, recv, old = ins[3 * u : 3 * u + 3]
        rows, width = old.shape
        mass = keep[rows : rows + 1, :] + recv[rows : rows + 1, :] + 1.0
        for out, which in ((mine_ref, z), (theirs_ref, 1 - z)):
            at = pl.ds(pl.multiple_of(which * (rows // 2), rows // 2), rows // 2)
            out[:, u * width : (u + 1) * width] = (keep[at, :] + recv[at, :] + old[at, :]) / mass


def last_update(me, triples):
    rows, width = triples[0][2].shape
    shape = jax.ShapeDtypeStruct((rows // 2, width * len(triples)), F32)
    flat = [a for t in triples for a in t]
    return pl.pallas_call(
        last_kernel,
        in_specs=[pl.BlockSpec(memory_space=pltpu.SMEM)]
        + [pl.BlockSpec(memory_space=pltpu.VMEM)] * len(flat),
        out_specs=[pl.BlockSpec(memory_space=pltpu.VMEM)] * 2,
        out_shape=[shape, shape],
        compiler_params=params(12),
        cost_estimate=cost(8 * rows * width, 32 * rows * width),
        name="last_update",
    )(me, *flat)


def weights_kernel(
    me_ref,
    own_ref,
    all_ref,
    e_ref,
    xh_ref,
    xl_ref,
    mine_ref,
    other_ref,
    out_ref,
    tick_ref,
    ch,
    cl,
    norm,
):
    me = me_ref[0]
    core, z = me & 1, me // 8

    @pl.when(pl.program_id(0) == 0)
    def _():
        rows = mine_ref.shape[0] // 8
        total = jnp.zeros((1, mine_ref.shape[1]), F32)
        for piece, side in ((mine_ref, core), (other_ref, 1 - core)):
            for j in range(8):
                v = piece[j * rows : (j + 1) * rows, :]
                hi, lo = split(v)
                x = (((me >> 1) & 3) - j // 2 + 4) & 3
                block = x * 2 + side + 8 * (j % 2)
                at = pl.ds(pl.multiple_of(block * rows, rows), rows)
                ch[at, :] = hi
                cl[at, :] = lo
                total = total + jnp.sum(v * v, axis=0, keepdims=True)
        norm[0:1, :] = 0.5 * total

    tops = all_ref[:, 0, :]
    top = jnp.max(tops, axis=0, keepdims=True)
    total = jnp.sum(all_ref[:, 1, :] * jnp.exp(tops - top), axis=0, keepdims=True)
    width = e_ref.shape[1]
    column = lambda v: jnp.broadcast_to(v, (128, v.shape[1])).T[:, 0:1]
    here = pl.ds(pl.multiple_of(z * width, width), width)
    there = pl.ds(pl.multiple_of((1 - z) * width, width), width)
    out_ref[:, here] = e_ref[...] * column(jnp.exp(own_ref[0:1, :] - top) / total)
    raw = dot3(xh_ref[...], xl_ref[...], ch[...], cl[...])
    logits = (raw - norm[0:1, :]) * 10.0
    out_ref[:, there] = jnp.exp(logits - column(top)) * column(1.0 / total)
    tick_ref[...] = norm[:, 0:128]


def final_weights(me, own, everyone, e_own, near, mine, other, tile=256):
    n, width = e_own.shape
    d = near[0].shape[1]
    t = n // tile
    rows = pl.BlockSpec((tile, d), lambda i, s: (i, 0))
    return pl.pallas_call(
        weights_kernel,
        grid_spec=pltpu.PrefetchScalarGridSpec(
            num_scalar_prefetch=1,
            grid=(t,),
            in_specs=[
                pl.BlockSpec((2, tile), lambda i, s: (0, (s[0] // 8) * t + i)),
                pl.BlockSpec(
                    (everyone.shape[0], 2, tile), lambda i, s: (0, 0, (s[0] // 8) * t + i)
                ),
                pl.BlockSpec((tile, width), lambda i, s: (i, 0)),
                rows,
                rows,
                NEAR,
                NEAR,
            ],
            out_specs=[pl.BlockSpec((tile, 2 * width), lambda i, s: (i, 0)), NEAR],
            scratch_shapes=[
                pltpu.VMEM((d, width), BF16),
                pltpu.VMEM((d, width), BF16),
                pltpu.VMEM((8, width), F32),
            ],
        ),
        out_shape=[pltpu.HBM((n, 2 * width), F32), jax.ShapeDtypeStruct((8, 128), F32)],
        compiler_params=params(24),
        cost_estimate=cost(6 * n * width * d, 4 * (n * d + 3 * n * width + d * width)),
        name="weights",
    )(me, own, everyone, e_own, *far_memory(*near), mine, other)


def local(x, c):
    index = lax.axis_index("pts").astype(jnp.int32)
    me = index.reshape(1)
    place_cen = lax.axis_index("cen").astype(jnp.int32)
    run, y = place_cen & 3, place_cen // 4
    at = jnp.stack([y * 2 + (run & 1), run >> 1, run, y])
    d, k = c.shape
    rows = d // 16
    cen = lax.axis_size("cen")
    orders = [relative_blocks(gens) for gens in COLORS]
    along_y = lambda v, shift: lax.ppermute(
        v, "cen", [(j, (j + 4 * shift) % cen) for j in range(cen)]
    )

    piece = own_piece(x, at)
    e, stats, copies, xh, xl, th, tl = first_step(me, at, piece, x, c, cen)
    piece = swap(piece, ZG)
    everyone = lax.all_to_all(copies, "cen", 0, 0)
    units, pin = [], piece
    for u, order in enumerate(orders):
        units.append(first_moments(me, pin, stats, everyone, th, tl, e, u, order))
        pin = units[-1][1]
    old = old_block(c, me, rows, k // 2, pin)
    other = lax.ppermute(relay(piece, units[0][1]), "cen", [(j, j ^ 1) for j in range(cen)])
    quarter = couple(at, old, piece, other)
    units = fold([(k_, swap(s_, g[0])) for g, (k_, s_) in zip(COLORS, units)])
    units = fold([(k_, swap(s_, g[1])) for g, (k_, s_) in zip(COLORS, units)], quarter)
    quarters = [quarter] + [along_y(quarter, shift) for shift in (1, 2, 3)]
    units = part([(k_, swap(s_, g[2])) for g, (k_, s_) in zip(COLORS, units)])
    units = [(k_, swap(s_, ZG)) for k_, s_ in units]
    *shares, joint = update(units, old, quarters[1], quarters[3])
    joint = swap(joint, ZG)
    cur = stack([(v, swap(v, g[2])) for g, v in zip(COLORS, shares)], quarters[2])
    fh, fl, gh, gl = far_points(at, quarters)
    cur = stack([(v, swap(v, g[1])) for g, v in zip(COLORS, cur)])
    pieces = [(v, swap(v, CORE)) for v in cur]
    e_own, stats, ch, cl, norm = own_logits(me, pieces, orders, (xh, xl))
    e_far, stats = far_logits(me, ch, cl, norm, stats, (fh, fl))
    everyone = lax.all_to_all(merge(joint, stats, swap(stats, ZG), cen), "cen", 0, 0)
    joint = relay(joint, everyone)
    peers = [joint]
    for shift in (1, 2, 3):
        to = [(i, (i & 9) | ((((i >> 1) + shift) & 3) << 1)) for i in range(16)]
        peers.append(lax.ppermute(joint, "pts", to))
    units, pin = [], everyone
    for u, order in enumerate(orders):
        units.append(
            next_moments(me, pin, stats, everyone, (th, tl), (gh, gl), e_own, e_far, u, order)
        )
        pin = units[-1][1]
    far_mine = column(peers, pin)
    for step in range(2):
        units = fold([(k_, swap(s_, g[step])) for g, (k_, s_) in zip(COLORS, units)])
    far_other = swap(far_mine, CORE)
    triples = [(k_, swap(s_, g[2]), o_) for g, (k_, s_), o_ in zip(COLORS, units, shares)]
    weights, tick = final_weights(me, stats, everyone, e_own, (xh, xl), far_mine, far_other)
    mine, theirs = last_update(me, triples)
    return weights, place(me, tick, mine, swap(theirs, ZG))


def place_kernel(me_ref, pin_ref, mine_ref, other_ref, out_ref):
    z = me_ref[0] // 8
    width = mine_ref.shape[1]
    out_ref[:, pl.ds(pl.multiple_of(z * width, width), width)] = mine_ref[...]
    out_ref[:, pl.ds(pl.multiple_of((1 - z) * width, width), width)] = other_ref[...]


def place(me, pin, mine, other):
    rows, width = mine.shape
    return pl.pallas_call(
        place_kernel,
        in_specs=[SMALL, ANY, NEAR, NEAR],
        out_specs=NEAR,
        out_shape=jax.ShapeDtypeStruct((rows, 2 * width), F32),
        compiler_params=params(4),
        cost_estimate=cost(1, 16 * rows * width),
        name="place",
    )(me, pin, mine, other)


def solution(mesh):
    placed = (P("pts", None), P(None, "cen"))
    return jax.shard_map(
        local,
        mesh=mesh,
        in_specs=placed,
        out_specs=(P("pts", "cen"), P("pts", "cen")),
        check_vma=False,
    )
```

```python
import functools

import jax
import jax.numpy as jnp
from jax import lax
from jax.experimental import pallas as pl
from jax.experimental.pallas import tpu as pltpu
from jax.sharding import PartitionSpec as P

F32 = jnp.float32
BF16 = jnp.bfloat16
PAD = 8
MIB = 1 << 20
CORE, XA, XB, ZG = 1, 2, 6, 8
X_PEERS = (2, 4, 6)
COLORS = ((CORE, XA, XB), (CORE, XB, XA))
COST = 0.1


def split(v):
    hi = v.astype(BF16)
    return hi, (v - hi.astype(F32)).astype(BF16)


def dot3(ah, al, bh, bl):
    dot = functools.partial(jnp.dot, preferred_element_type=F32)
    return dot(ah, bh) + (dot(ah, bl) + dot(al, bh))


def swap(v, g):
    return lax.ppermute(v, "pts", [(i, i ^ g) for i in range(lax.axis_size("pts"))])


def relative_blocks(gens):
    out = [0]
    for g in reversed(gens):
        out = out + [r ^ g for r in out]
    return out


def params(mib):
    return pltpu.CompilerParams(vmem_limit_bytes=mib * MIB)


def cost(flops, nbytes):
    return pl.CostEstimate(
        flops=int(flops * COST), bytes_accessed=int(nbytes * COST), transcendentals=0
    )


def far_memory(*arrays):
    out = [pltpu.with_memory_space_constraint(a, pltpu.HBM) for a in arrays]
    return out[0] if len(out) == 1 else out


def near_memory(*arrays):
    return [pltpu.with_memory_space_constraint(a, pltpu.VMEM) for a in arrays]


ANY = pl.BlockSpec(memory_space=pl.ANY)
SMALL = pl.BlockSpec(memory_space=pltpu.SMEM)
NEAR = pl.BlockSpec(memory_space=pltpu.VMEM)


def whole(a):
    return pl.BlockSpec(a.shape, lambda i, s: (0,) * len(a.shape))


def softmax_part(raw_ref, half_norm, e_ref, at):
    logits = (raw_ref[...] - half_norm) * 10.0
    top = jnp.max(logits, axis=1, keepdims=True)
    expo = jnp.exp(logits - top)
    total = jnp.sum(expo, axis=1, keepdims=True)
    e_ref[at, :] = expo
    row = lambda v: jnp.broadcast_to(v, (v.shape[0], 128)).T[0:1, :]
    return row(top), row(total)


def tiled(tiles, product, finish, raws):
    for i in range(tiles + 1):
        if i < tiles:
            raws[i % 2][...] = product(i)
        if i > 0:
            finish(i - 1, raws[(i - 1) % 2])


def put_stats(stats, stat_ref, all_ref, at):
    for i, v in enumerate(stats):
        stat_ref[i : i + 1, at] = v
        all_ref[:, i : i + 1, at] = jnp.broadcast_to(v[None], (all_ref.shape[0], *v.shape))


def first_kernel(
    me_ref,
    at_ref,
    pin_ref,
    x_ref,
    c_ref,
    e_ref,
    stat_ref,
    all_ref,
    xh_ref,
    xl_ref,
    th_ref,
    tl_ref,
    xs,
    cs,
    ch,
    cl,
    raw0,
    raw1,
    sems,
):
    tile = raw0.shape[0]
    tiles = x_ref.shape[0] // tile
    chunks = sems.shape[0] - tiles
    step = c_ref.shape[0] // chunks
    c_at = [pl.ds(j * step, step) for j in range(chunks)]
    x_at = [pl.ds(j * tile, tile) for j in range(tiles)]
    c_in = [
        pltpu.make_async_copy(c_ref.at[at, :], cs.at[at, :], sems.at[j])
        for j, at in enumerate(c_at)
    ]
    x_in = [
        pltpu.make_async_copy(x_ref.at[at, :], xs.at[at, :], sems.at[chunks + j])
        for j, at in enumerate(x_at)
    ]
    for copy in c_in + x_in:
        copy.start()
    total = jnp.zeros((1, cs.shape[1]), F32)
    for copy, at in zip(c_in, c_at):
        copy.wait()
        v = cs[at, :]
        ch[at, :], cl[at, :] = split(v)
        total = total + jnp.sum(v * v, axis=0, keepdims=True)
    half_norm = 0.5 * total

    def product(i):
        at = x_at[i]
        x_in[i].wait()
        x = xs[at, :]
        hi, lo = split(x)
        xh_ref[at, :] = hi
        xl_ref[at, :] = lo
        th_ref[:, at], tl_ref[:, at] = split(x.T)
        return dot3(hi, lo, ch[...], cl[...])

    def finish(i, raw):
        put_stats(softmax_part(raw, half_norm, e_ref, x_at[i]), stat_ref, all_ref, x_at[i])

    tiled(tiles, product, finish, (raw0, raw1))


def first_step(me, at, pin, x, c, copies, tile=256, chunks=8):
    n, d = x.shape
    k = c.shape[1]
    return pl.pallas_call(
        first_kernel,
        in_specs=[SMALL, SMALL, ANY, ANY, ANY],
        out_specs=[NEAR] * 7,
        out_shape=[
            pltpu.VMEM((n, k), F32),
            jax.ShapeDtypeStruct((2, n), F32),
            jax.ShapeDtypeStruct((copies, 2, n), F32),
            pltpu.VMEM((n, d), BF16),
            pltpu.VMEM((n, d), BF16),
            pltpu.VMEM((d, n), BF16),
            pltpu.VMEM((d, n), BF16),
        ],
        scratch_shapes=[
            pltpu.VMEM((n, d), F32),
            pltpu.VMEM((d, k), F32),
            pltpu.VMEM((d, k), BF16),
            pltpu.VMEM((d, k), BF16),
            pltpu.VMEM((tile, k), F32),
            pltpu.VMEM((tile, k), F32),
            pltpu.SemaphoreType.DMA((chunks + n // tile,)),
        ],
        compiler_params=params(36),
        cost_estimate=cost(20 * 6 * n * d * k, 4 * (2 * n * d + d * k + n * k)),
        name="first_logits",
    )(me, at, pin, *far_memory(x, c))


def far_kernel(at_ref, *refs):
    pieces, (xh_ref, xl_ref, th_ref, tl_ref) = refs[:4], refs[4:]
    width = pieces[0].shape[1]
    for shift, piece in enumerate(pieces):
        quarter = lax.rem(at_ref[3] - shift + 4, 4)
        at = pl.ds(pl.multiple_of(quarter * width, width), width)
        v = piece[...]
        xh_ref[:, at], xl_ref[:, at] = split(v)
        th_ref[at, :], tl_ref[at, :] = split(v.T)


def far_points(at, pieces):
    n, width = pieces[0].shape
    d = width * len(pieces)
    return pl.pallas_call(
        far_kernel,
        in_specs=[SMALL] + [NEAR] * len(pieces),
        out_specs=[NEAR] * 4,
        out_shape=[pltpu.VMEM(s, BF16) for s in ((n, d), (n, d), (d, n), (d, n))],
        compiler_params=params(16),
        cost_estimate=cost(4 * n * d, 12 * n * d),
        name="far_points",
    )(at, *pieces)


def slice_kernel(at_ref, pin_ref, x_ref, out_ref):
    out_ref[...] = x_ref[...]


def own_piece(x, at):
    n, size = x.shape[0], x.shape[1] // 8
    return pl.pallas_call(
        lambda at_ref, x_ref, out_ref: slice_kernel(at_ref, None, x_ref, out_ref),
        grid_spec=pltpu.PrefetchScalarGridSpec(
            num_scalar_prefetch=1,
            grid=(1,),
            in_specs=[pl.BlockSpec((n, size), lambda i, s: (0, s[0]))],
            out_specs=pl.BlockSpec((n, size), lambda i, s: (0, 0)),
        ),
        out_shape=jax.ShapeDtypeStruct((n, size), F32),
        compiler_params=params(8),
        cost_estimate=cost(1, 8 * n * size),
        name="own_piece",
    )(at, far_memory(x))


def couple_kernel(at_ref, pin_ref, mine_ref, other_ref, out_ref):
    width = mine_ref.shape[1]
    side = at_ref[0] & 1
    out_ref[:, pl.ds(pl.multiple_of(side * width, width), width)] = mine_ref[...]
    out_ref[:, pl.ds(pl.multiple_of((1 - side) * width, width), width)] = other_ref[...]


def couple(at, pin, mine, other):
    n, width = mine.shape
    return pl.pallas_call(
        couple_kernel,
        in_specs=[SMALL, ANY, NEAR, NEAR],
        out_specs=NEAR,
        out_shape=jax.ShapeDtypeStruct((n, 2 * width), F32),
        compiler_params=params(4),
        cost_estimate=cost(1, 16 * n * width),
        name="couple",
    )(at, pin, mine, other)


def old_block(c, me, rows, width, pin):
    return pl.pallas_call(
        slice_kernel,
        grid_spec=pltpu.PrefetchScalarGridSpec(
            num_scalar_prefetch=1,
            grid=(2,),
            in_specs=[
                ANY,
                pl.BlockSpec((rows, width), lambda b, s: ((s[0] & 7) + 8 * b, s[0] // 8)),
            ],
            out_specs=pl.BlockSpec((rows, width), lambda b, s: (b, 0)),
        ),
        out_shape=jax.ShapeDtypeStruct((2 * rows, width), F32),
        compiler_params=params(4),
        cost_estimate=cost(1, 16 * rows * width),
        name="old_block",
    )(me, pin, far_memory(c))


def spread(me, sides, ch, cl):
    total = jnp.zeros((1, ch.shape[1]), F32)
    for side, pieces in sides:
        rows = pieces[0].shape[0] // 2
        for mask, piece in zip((0, *X_PEERS), pieces):
            for z in range(2):
                v = piece[z * rows : (z + 1) * rows, :]
                hi, lo = split(v)
                at = (((me ^ mask ^ side) & 7) + 8 * z) * rows
                at = pl.ds(pl.multiple_of(at, rows), rows)
                ch[at, :] = hi
                cl[at, :] = lo
                total = total + jnp.sum(v * v, axis=0, keepdims=True)
    return 0.5 * total


def quarters_of(ref):
    rows = ref.shape[0] // 4
    return [ref.at[pl.ds(j * rows, rows), :] for j in range(4)]


def own_kernel(me_ref, mine_ref, other_ref, xh, xl, e_ref, stat_ref, ch, cl, norm, raw0, raw1):
    me = me_ref[0]
    half_norm = spread(
        me, ((0, quarters_of(mine_ref)), (CORE, quarters_of(other_ref))), ch, cl
    )
    norm[...] = jnp.broadcast_to(half_norm, norm.shape)
    tile = raw0.shape[0]

    def finish(i, raw):
        at = pl.ds(i * tile, tile)
        for j, v in enumerate(softmax_part(raw, half_norm, e_ref, at)):
            stat_ref[j : j + 1, at] = v

    product = lambda i: dot3(
        xh[pl.ds(i * tile, tile), :], xl[pl.ds(i * tile, tile), :], ch[...], cl[...]
    )
    tiled(xh.shape[0] // tile, product, finish, (raw0, raw1))


def own_logits(me, mine, other, near, tile=256):
    n, d = near[0].shape
    k = mine.shape[1]
    return pl.pallas_call(
        own_kernel,
        in_specs=[SMALL] + [NEAR] * 4,
        out_specs=[NEAR] * 5,
        out_shape=[
            pltpu.VMEM((n, k), F32),
            jax.ShapeDtypeStruct((2, n), F32),
            pltpu.VMEM((d, k), BF16),
            pltpu.VMEM((d, k), BF16),
            pltpu.VMEM((8, k), F32),
        ],
        scratch_shapes=[pltpu.VMEM((tile, k), F32)] * 2,
        compiler_params=params(20),
        cost_estimate=cost(6 * n * d * k, 4 * (n * d + d * k + n * k)),
        name="own_logits",
    )(me, mine, other, *near)


def far_logits_kernel(me_ref, ch, cl, norm, own_ref, xh, xl, e_ref, stat_ref, raw0, raw1):
    tile = raw0.shape[0]
    n = own_ref.shape[1]
    z = me_ref[0] // 8
    stat_ref[:, pl.ds(pl.multiple_of(z * n, n), n)] = own_ref[...]

    def finish(i, raw):
        at = pl.ds(pl.multiple_of((1 - z) * n + i * tile, tile), tile)
        stats = softmax_part(raw, norm[0:1, :], e_ref, pl.ds(i * tile, tile))
        for j, v in enumerate(stats):
            stat_ref[j : j + 1, at] = v

    product = lambda i: dot3(
        xh[pl.ds(i * tile, tile), :], xl[pl.ds(i * tile, tile), :], ch[...], cl[...]
    )
    tiled(n // tile, product, finish, (raw0, raw1))


def far_logits(me, ch, cl, norm, own, far, tile=256):
    n, d = far[0].shape
    k = ch.shape[1]
    return pl.pallas_call(
        far_logits_kernel,
        in_specs=[SMALL] + [NEAR] * 6,
        out_specs=[NEAR] * 2,
        out_shape=[pltpu.VMEM((n, k), F32), jax.ShapeDtypeStruct((2, 2 * n), F32)],
        scratch_shapes=[pltpu.VMEM((tile, k), F32)] * 2,
        compiler_params=params(16),
        cost_estimate=cost(6 * n * d * k, 4 * (n * d + d * k + n * k)),
        name="far_logits",
    )(me, ch, cl, norm, own, *far)


def merge_kernel(pin_ref, mine_ref, other_ref, out_ref):
    top = jnp.maximum(mine_ref[0:1, :], other_ref[0:1, :])
    total = sum(ref[1:2, :] * jnp.exp(ref[0:1, :] - top) for ref in (mine_ref, other_ref))
    for i, v in enumerate((top, total)):
        out_ref[:, i : i + 1, :] = jnp.broadcast_to(v[None], (out_ref.shape[0], *v.shape))


def merge(pin, mine, other, copies):
    return pl.pallas_call(
        merge_kernel,
        in_specs=[ANY, NEAR, NEAR],
        out_specs=NEAR,
        out_shape=jax.ShapeDtypeStruct((copies, *mine.shape), F32),
        compiler_params=params(4),
        cost_estimate=cost(copies * mine.size, 8 * copies * mine.size),
        name="merge",
    )(pin, mine, other)


def row_scale(own, everyone):
    tops = everyone[:, 0, :]
    top = jnp.max(tops, axis=0, keepdims=True)
    total = jnp.sum(everyone[:, 1, :] * jnp.exp(tops - top), axis=0, keepdims=True)
    scale = jnp.exp(own[0:1, :] - top) / total
    return jnp.broadcast_to(scale, (128, scale.shape[1])).T[:, 0:1]


def permuted(order, low, ref, out):
    rows = ref.shape[0] // (2 * len(order))
    for j, r in enumerate(order):
        for b in range(2):
            at = pl.ds(pl.multiple_of(((low ^ r) + 8 * b) * rows, rows), rows)
            out[(2 * j + b) * rows : (2 * j + b + 1) * rows, :] = ref[at, :]


def emit(m, w, keep_ref, send_ref, at):
    half = m.shape[0] // 2
    mass = jnp.broadcast_to(jnp.sum(w, axis=0, keepdims=True), (PAD, w.shape[1]))
    keep_ref[0:half, at] = m[:half]
    send_ref[0:half, at] = m[half:]
    keep_ref[half : half + PAD, at] = mass
    send_ref[half : half + PAD, at] = mass


def first_moment_kernel(
    order, color, me_ref, pin_ref, own_ref, all_ref, th_ref, tl_ref, e_ref, keep_ref, send_ref, ph, pt
):
    low, z = me_ref[0] & 7, me_ref[0] // 8
    permuted(order, low, th_ref, ph)
    permuted(order, low, tl_ref, pt)
    scale = row_scale(own_ref[...], all_ref[...])
    width = e_ref.shape[1] // 4
    for h in range(2):
        column = pl.multiple_of((2 * (z ^ h) + color) * width, width)
        w = e_ref[:, pl.ds(column, width)] * scale
        wh, wl = split(w)
        m = dot3(ph[...], pt[...], wh, wl)
        emit(m, w, keep_ref, send_ref, slice(h * width, (h + 1) * width))


def first_moments(me, pin, own, everyone, th, tl, e, color, order):
    d, n = th.shape
    width = e.shape[1] // 4
    shape = jax.ShapeDtypeStruct((d // 2 + PAD, 2 * width), F32)
    return pl.pallas_call(
        functools.partial(first_moment_kernel, order, color),
        in_specs=[SMALL, ANY] + [NEAR] * 5,
        out_specs=[NEAR, NEAR],
        out_shape=[shape, shape],
        scratch_shapes=[pltpu.VMEM((d, n), BF16), pltpu.VMEM((d, n), BF16)],
        compiler_params=params(20),
        cost_estimate=cost(12 * d * n * width, 4 * (d * n + 2 * n * width + 2 * d * width)),
        name="first_moments",
    )(me, pin, own, everyone, th, tl, e)


def next_moment_kernel(
    order, color, me_ref, pin_ref, own, everyone, oh, ol, gh, gl, e0, e1, keep_ref, send_ref, ph, pt
):
    low, z = me_ref[0] & 7, me_ref[0] // 8
    n = e0.shape[0]
    width = e0.shape[1] // 2
    m = w_all = None
    for h, (th, tl, e) in enumerate(((oh, ol, e0), (gh, gl, e1))):
        at = pl.ds(pl.multiple_of((z ^ h) * n, n), n)
        permuted(order, low, th, ph)
        permuted(order, low, tl, pt)
        w = e[:, color * width : (color + 1) * width] * row_scale(own[:, at], everyone[:, :, at])
        wh, wl = split(w)
        part = dot3(ph[...], pt[...], wh, wl)
        m, w_all = (part, w) if m is None else (m + part, w_all + w)
    emit(m, w_all, keep_ref, send_ref, slice(None))


def next_moments(me, pin, own, everyone, near, far, e_own, e_far, color, order):
    d, n = near[0].shape
    width = e_own.shape[1] // 2
    shape = jax.ShapeDtypeStruct((d // 2 + PAD, width), F32)
    return pl.pallas_call(
        functools.partial(next_moment_kernel, order, color),
        in_specs=[SMALL, ANY] + [NEAR] * 8,
        out_specs=[NEAR, NEAR],
        out_shape=[shape, shape],
        scratch_shapes=[pltpu.VMEM((d, n), BF16)] * 2,
        compiler_params=params(20),
        cost_estimate=cost(12 * d * n * width, 4 * (2 * d * n + 2 * n * width + d * width)),
        name="next_moments",
    )(me, pin, own, everyone, *near, *far, e_own, e_far)


def relay_kernel(pin_ref, in_ref, out_ref):
    pass


def relay(a, pin):
    return pl.pallas_call(
        relay_kernel,
        in_specs=[ANY, ANY],
        out_specs=ANY,
        out_shape=jax.ShapeDtypeStruct(a.shape, a.dtype),
        input_output_aliases={1: 0},
        compiler_params=params(4),
        cost_estimate=cost(1, 1),
        name="relay",
    )(pin, a)


def chain(kernel, name, ins, shapes, pins=()):
    size = sum(a.size for a in ins)
    return pl.pallas_call(
        kernel,
        in_specs=[ANY] * len(pins) + [NEAR] * len(ins),
        out_shape=[jax.ShapeDtypeStruct(shape, F32) for shape in shapes],
        compiler_params=params(16),
        cost_estimate=cost(size, 8 * size),
        name=name,
    )(*pins, *ins)


def fold_kernel(pins, *refs):
    refs = refs[pins:]
    count = len(refs) // 4
    for u in range(count):
        keep, recv = refs[2 * u : 2 * u + 2]
        out, send = refs[2 * (count + u) : 2 * (count + u) + 2]
        half = (keep.shape[0] - PAD) // 2
        out[0:half, :] = keep[0:half, :] + recv[0:half, :]
        send[0:half, :] = keep[half : 2 * half, :] + recv[half : 2 * half, :]
        mass = keep[2 * half :, :] + recv[2 * half :, :]
        out[half:, :] = mass
        send[half:, :] = mass


def fold(ins, *pins):
    shapes = []
    for keep, _ in ins:
        shapes += [((keep.shape[0] - PAD) // 2 + PAD, keep.shape[1])] * 2
    kernel = functools.partial(fold_kernel, len(pins))
    flat = chain(kernel, "fold", [a for pair in ins for a in pair], shapes, pins)
    return [(flat[2 * i], flat[2 * i + 1]) for i in range(len(ins))]


def part_kernel(*refs):
    ins, (out, send) = refs[:-2], refs[-2:]
    for u in range(len(ins) // 2):
        keep, recv = ins[2 * u : 2 * u + 2]
        half = keep.shape[1] // 2
        cols = slice(u * half, (u + 1) * half)
        out[:, cols] = keep[:, 0:half] + recv[:, 0:half]
        send[:, cols] = keep[:, half:] + recv[:, half:]


def part(ins):
    rows, width = ins[0][0].shape
    shape = (rows, width // 2 * len(ins))
    return chain(part_kernel, "part", [a for pair in ins for a in pair], [shape] * 2)


def update_kernel(pins, *refs):
    keep, recv, old, out = refs[pins:]
    rows = old.shape[0]
    mass = keep[rows : rows + 1, :] + recv[rows : rows + 1, :] + 1.0
    out[...] = (keep[0:rows, :] + recv[0:rows, :] + old[...]) / mass


def update(keep, recv, old, *pins):
    kernel = functools.partial(update_kernel, len(pins))
    return chain(kernel, "update", [keep, recv, old], [old.shape], pins)[0]


def column_kernel(pins, *refs):
    refs = refs[pins:]
    rows = refs[0].shape[0]
    for i, ref in enumerate(refs[:-1]):
        refs[-1][i * rows : (i + 1) * rows, :] = ref[...]


def column(pieces, *pins):
    rows, width = pieces[0].shape
    kernel = functools.partial(column_kernel, len(pins))
    return chain(kernel, "column", pieces, [(rows * len(pieces), width)], pins)[0]


def last_kernel(me_ref, old, *refs):
    ins, (mine_ref, theirs_ref) = refs[:-2], refs[-2:]
    z = me_ref[0] // 8
    rows = old.shape[0]
    for u in range(len(ins) // 2):
        keep, recv = ins[2 * u : 2 * u + 2]
        cols = slice(u * keep.shape[1], (u + 1) * keep.shape[1])
        mass = keep[rows : rows + 1, :] + recv[rows : rows + 1, :] + 1.0
        for out, which in ((mine_ref, z), (theirs_ref, 1 - z)):
            at = pl.ds(pl.multiple_of(which * (rows // 2), rows // 2), rows // 2)
            out[:, cols] = (keep[at, :] + recv[at, :] + old[at, cols]) / mass


def last_update(me, ins, old):
    rows, width = old.shape
    shape = jax.ShapeDtypeStruct((rows // 2, width), F32)
    flat = [a for pair in ins for a in pair]
    return pl.pallas_call(
        last_kernel,
        in_specs=[SMALL] + [NEAR] * (1 + len(flat)),
        out_specs=[NEAR] * 2,
        out_shape=[shape, shape],
        compiler_params=params(16),
        cost_estimate=cost(8 * rows * width, 32 * rows * width),
        name="last_update",
    )(me, old, *flat)


def weights_kernel(
    me_ref,
    own_ref,
    all_ref,
    e_ref,
    xh_ref,
    xl_ref,
    mine_ref,
    other_ref,
    out_ref,
    tick_ref,
    ch,
    cl,
    norm,
):
    me = me_ref[0]
    z = me // 8

    @pl.when(pl.program_id(0) == 0)
    def _():
        sides = (0, quarters_of(mine_ref)), (CORE, quarters_of(other_ref))
        norm[...] = jnp.broadcast_to(spread(me, sides, ch, cl), norm.shape)

    tops = all_ref[:, 0, :]
    top = jnp.max(tops, axis=0, keepdims=True)
    total = jnp.sum(all_ref[:, 1, :] * jnp.exp(tops - top), axis=0, keepdims=True)
    width = e_ref.shape[1]
    column = lambda v: jnp.broadcast_to(v, (128, v.shape[1])).T[:, 0:1]
    here = pl.ds(pl.multiple_of(z * width, width), width)
    there = pl.ds(pl.multiple_of((1 - z) * width, width), width)
    out_ref[:, here] = e_ref[...] * column(jnp.exp(own_ref[0:1, :] - top) / total)
    raw = dot3(xh_ref[...], xl_ref[...], ch[...], cl[...])
    logits = (raw - norm[0:1, :]) * 10.0
    out_ref[:, there] = jnp.exp(logits - column(top)) * column(1.0 / total)
    tick_ref[...] = norm[:, 0:128]


def final_weights(me, own, everyone, e_own, near, mine, other, tile=256):
    n, width = e_own.shape
    d = near[0].shape[1]
    t = n // tile
    rows = pl.BlockSpec((tile, d), lambda i, s: (i, 0))
    return pl.pallas_call(
        weights_kernel,
        grid_spec=pltpu.PrefetchScalarGridSpec(
            num_scalar_prefetch=1,
            grid=(t,),
            in_specs=[
                pl.BlockSpec((2, tile), lambda i, s: (0, (s[0] // 8) * t + i)),
                pl.BlockSpec(
                    (everyone.shape[0], 2, tile), lambda i, s: (0, 0, (s[0] // 8) * t + i)
                ),
                pl.BlockSpec((tile, width), lambda i, s: (i, 0)),
                rows,
                rows,
                NEAR,
                NEAR,
            ],
            out_specs=[pl.BlockSpec((tile, 2 * width), lambda i, s: (i, 0)), NEAR],
            scratch_shapes=[
                pltpu.VMEM((d, width), BF16),
                pltpu.VMEM((d, width), BF16),
                pltpu.VMEM((8, width), F32),
            ],
        ),
        out_shape=[pltpu.HBM((n, 2 * width), F32), jax.ShapeDtypeStruct((8, 128), F32)],
        compiler_params=params(24),
        cost_estimate=cost(6 * n * width * d, 4 * (n * d + 3 * n * width + d * width)),
        name="weights",
    )(me, own, everyone, e_own, *near, mine, other)


def local(x, c):
    index = lax.axis_index("pts").astype(jnp.int32)
    me = index.reshape(1)
    place_cen = lax.axis_index("cen").astype(jnp.int32)
    run, y = place_cen & 3, place_cen // 4
    at = jnp.stack([y * 2 + (run & 1), run >> 1, run, y])
    d, k = c.shape
    rows = d // 16
    cen = lax.axis_size("cen")
    along_y = lambda v, shift: lax.ppermute(
        v, "cen", [(j, (j + 4 * shift) % cen) for j in range(cen)]
    )

    piece = own_piece(x, at)
    e, stats, copies, xh, xl, th, tl = first_step(me, at, piece, x, c, cen)
    piece = swap(piece, ZG)
    everyone = lax.all_to_all(copies, "cen", 0, 0)
    orders = [relative_blocks(gens) for gens in COLORS]
    swapped = lambda units, step: [
        (keep, swap(send, gens[step])) for gens, (keep, send) in zip(COLORS, units)
    ]
    units, pin = [], piece
    for u, order in enumerate(orders):
        units.append(first_moments(me, pin, stats, everyone, th, tl, e, u, order))
        pin = units[-1][1]
    old = old_block(c, me, rows, k // 2, pin)
    other = lax.ppermute(relay(piece, units[0][1]), "cen", [(j, j ^ 1) for j in range(cen)])
    quarter = couple(at, old, piece, other)
    units = fold(swapped(units, 0))
    units = fold(swapped(units, 1), quarter)
    quarters = [quarter] + [along_y(quarter, shift) for shift in (1, 2, 3)]
    keep, send = part(swapped(units, 2))
    share = update(keep, swap(send, ZG), old)
    joint = swap(share, ZG)
    mine = column([share] + [swap(share, mask) for mask in X_PEERS], *quarters[1:])
    fh, fl, gh, gl = far_points(at, quarters)
    e_own, stats, ch, cl, norm = own_logits(me, mine, swap(mine, CORE), (xh, xl))
    e_far, stats = far_logits(me, ch, cl, norm, stats, (fh, fl))
    everyone = lax.all_to_all(merge(joint, stats, swap(stats, ZG), cen), "cen", 0, 0)
    joint = relay(joint, everyone)
    peers = [joint] + [swap(joint, mask) for mask in X_PEERS]
    units, pin = [], everyone
    for u, order in enumerate(orders):
        units.append(
            next_moments(me, pin, stats, everyone, (th, tl), (gh, gl), e_own, e_far, u, order)
        )
        pin = units[-1][1]
    far_mine = column(peers, pin)
    units = fold(swapped(units, 0))
    units = fold(swapped(units, 1))
    far_other = swap(far_mine, CORE)
    weights, tick = final_weights(me, stats, everyone, e_own, (xh, xl), far_mine, far_other)
    mine, theirs = last_update(me, swapped(units, 2), share)
    return weights, place(me, tick, mine, swap(theirs, ZG))


def place_kernel(me_ref, pin_ref, mine_ref, other_ref, out_ref):
    z = me_ref[0] // 8
    width = mine_ref.shape[1]
    out_ref[:, pl.ds(pl.multiple_of(z * width, width), width)] = mine_ref[...]
    out_ref[:, pl.ds(pl.multiple_of((1 - z) * width, width), width)] = other_ref[...]


def place(me, pin, mine, other):
    rows, width = mine.shape
    return pl.pallas_call(
        place_kernel,
        in_specs=[SMALL, ANY, NEAR, NEAR],
        out_specs=NEAR,
        out_shape=jax.ShapeDtypeStruct((rows, 2 * width), F32),
        compiler_params=params(4),
        cost_estimate=cost(1, 16 * rows * width),
        name="place",
    )(me, pin, mine, other)


def solution(mesh):
    placed = (P("pts", None), P(None, "cen"))
    return jax.shard_map(
        local,
        mesh=mesh,
        in_specs=placed,
        out_specs=(P("pts", "cen"), P("pts", "cen")),
        check_vma=False,
    )
```

```python
import functools

import jax
import jax.numpy as jnp
from jax import lax
from jax.experimental import pallas as pl
from jax.experimental.pallas import tpu as pltpu
from jax.sharding import PartitionSpec as P

F32 = jnp.float32
BF16 = jnp.bfloat16
PAD = 8
MIB = 1 << 20
CORE, XA, XB, ZG = 1, 2, 6, 8
X_PEERS = (2, 4, 6)
COLORS = ((CORE, XA, XB), (CORE, XB, XA))
COST = 0.1


def split(v):
    hi = v.astype(BF16)
    return hi, (v - hi.astype(F32)).astype(BF16)


def dot3(ah, al, bh, bl):
    dot = functools.partial(jnp.dot, preferred_element_type=F32)
    return dot(ah, bh) + (dot(ah, bl) + dot(al, bh))


def swap(v, g):
    return lax.ppermute(v, "pts", [(i, i ^ g) for i in range(lax.axis_size("pts"))])


def relative_blocks(gens):
    out = [0]
    for g in reversed(gens):
        out = out + [r ^ g for r in out]
    return out


def params(mib):
    return pltpu.CompilerParams(vmem_limit_bytes=mib * MIB)


def cost(flops, nbytes):
    return pl.CostEstimate(
        flops=int(flops * COST), bytes_accessed=int(nbytes * COST), transcendentals=0
    )


def far_memory(*arrays):
    out = [pltpu.with_memory_space_constraint(a, pltpu.HBM) for a in arrays]
    return out[0] if len(out) == 1 else out


def near_memory(*arrays):
    return [pltpu.with_memory_space_constraint(a, pltpu.VMEM) for a in arrays]


ANY = pl.BlockSpec(memory_space=pl.ANY)
SMALL = pl.BlockSpec(memory_space=pltpu.SMEM)
NEAR = pl.BlockSpec(memory_space=pltpu.VMEM)


def whole(a):
    return pl.BlockSpec(a.shape, lambda i, s: (0,) * len(a.shape))


def softmax_part(raw_ref, half_norm, e_ref, at):
    logits = (raw_ref[...] - half_norm) * 10.0
    top = jnp.max(logits, axis=1, keepdims=True)
    expo = jnp.exp(logits - top)
    total = jnp.sum(expo, axis=1, keepdims=True)
    e_ref[at, :] = expo
    row = lambda v: jnp.broadcast_to(v, (v.shape[0], 128)).T[0:1, :]
    return row(top), row(total)


def tiled3(tiles, product, finish, raws):
    for i in range(tiles + 1):
        if i < tiles:
            raws[i % 2][...] = product(i)
        if i > 0:
            finish(i - 1, raws[(i - 1) % 2])


def tiled(tiles, product, finish, raws):
    @pl.loop(0, tiles)
    def _(i):
        raws[0][...] = product(i)
        finish(i, raws[0])


def put_stats(stats, stat_ref, all_ref, at):
    for i, v in enumerate(stats):
        stat_ref[i : i + 1, at] = v
        all_ref[:, i : i + 1, at] = jnp.broadcast_to(v[None], (all_ref.shape[0], *v.shape))


def first_kernel(
    me_ref,
    at_ref,
    pin_ref,
    x_ref,
    c_ref,
    e_ref,
    stat_ref,
    all_ref,
    xh_ref,
    xl_ref,
    th_ref,
    tl_ref,
    xs,
    cs,
    ch,
    cl,
    raw0,
    raw1,
    sems,
):
    tile = raw0.shape[0]
    tiles = x_ref.shape[0] // tile
    chunks = sems.shape[0] - tiles
    step = c_ref.shape[0] // chunks
    c_at = [pl.ds(j * step, step) for j in range(chunks)]
    x_at = [pl.ds(j * tile, tile) for j in range(tiles)]
    c_in = [
        pltpu.make_async_copy(c_ref.at[at, :], cs.at[at, :], sems.at[j])
        for j, at in enumerate(c_at)
    ]
    x_in = [
        pltpu.make_async_copy(x_ref.at[at, :], xs.at[at, :], sems.at[chunks + j])
        for j, at in enumerate(x_at)
    ]
    for copy in c_in + x_in:
        copy.start()
    total = jnp.zeros((1, cs.shape[1]), F32)
    def arrived(j, total):
        at = pl.ds(pl.multiple_of(j * step, step), step)
        pltpu.make_async_copy(c_ref.at[at, :], cs.at[at, :], sems.at[j]).wait()
        v = cs[at, :]
        ch[at, :], cl[at, :] = split(v)
        return total + jnp.sum(v * v, axis=0, keepdims=True)

    total = lax.fori_loop(0, chunks, arrived, total)
    half_norm = 0.5 * total

    def product(i):
        at = x_at[i]
        x_in[i].wait()
        x = xs[at, :]
        hi, lo = split(x)
        xh_ref[at, :] = hi
        xl_ref[at, :] = lo
        th_ref[:, at], tl_ref[:, at] = split(x.T)
        return dot3(hi, lo, ch[...], cl[...])

    def finish(i, raw):
        put_stats(softmax_part(raw, half_norm, e_ref, x_at[i]), stat_ref, all_ref, x_at[i])

    tiled3(tiles, product, finish, (raw0, raw1))


def first_step(me, at, pin, x, c, copies, tile=256, chunks=8):
    n, d = x.shape
    k = c.shape[1]
    return pl.pallas_call(
        first_kernel,
        in_specs=[SMALL, SMALL, ANY, ANY, ANY],
        out_specs=[NEAR] * 7,
        out_shape=[
            pltpu.VMEM((n, k), F32),
            jax.ShapeDtypeStruct((2, n), F32),
            jax.ShapeDtypeStruct((copies, 2, n), F32),
            pltpu.VMEM((n, d), BF16),
            pltpu.VMEM((n, d), BF16),
            pltpu.VMEM((d, n), BF16),
            pltpu.VMEM((d, n), BF16),
        ],
        scratch_shapes=[
            pltpu.VMEM((n, d), F32),
            pltpu.VMEM((d, k), F32),
            pltpu.VMEM((d, k), BF16),
            pltpu.VMEM((d, k), BF16),
            pltpu.VMEM((tile, k), F32),
            pltpu.VMEM((tile, k), F32),
            pltpu.SemaphoreType.DMA((chunks + n // tile,)),
        ],
        compiler_params=params(36),
        cost_estimate=cost(20 * 6 * n * d * k, 4 * (2 * n * d + d * k + n * k)),
        name="first_logits",
    )(me, at, pin, *far_memory(x, c))


def far_kernel(at_ref, *refs):
    pieces, (xh_ref, xl_ref, th_ref, tl_ref) = refs[:4], refs[4:]
    width = pieces[0].shape[1]
    for shift, piece in enumerate(pieces):
        quarter = lax.rem(at_ref[3] - shift + 4, 4)
        at = pl.ds(pl.multiple_of(quarter * width, width), width)
        v = piece[...]
        xh_ref[:, at], xl_ref[:, at] = split(v)
        th_ref[at, :], tl_ref[at, :] = split(v.T)


def far_points(at, pieces):
    n, width = pieces[0].shape
    d = width * len(pieces)
    return pl.pallas_call(
        far_kernel,
        in_specs=[SMALL] + [NEAR] * len(pieces),
        out_specs=[NEAR] * 4,
        out_shape=[pltpu.VMEM(s, BF16) for s in ((n, d), (n, d), (d, n), (d, n))],
        compiler_params=params(16),
        cost_estimate=cost(4 * n * d, 12 * n * d),
        name="far_points",
    )(at, *pieces)


def slice_kernel(at_ref, pin_ref, x_ref, out_ref):
    out_ref[...] = x_ref[...]


def own_piece(x, at):
    n, size = x.shape[0], x.shape[1] // 8
    return pl.pallas_call(
        lambda at_ref, x_ref, out_ref: slice_kernel(at_ref, None, x_ref, out_ref),
        grid_spec=pltpu.PrefetchScalarGridSpec(
            num_scalar_prefetch=1,
            grid=(1,),
            in_specs=[pl.BlockSpec((n, size), lambda i, s: (0, s[0]))],
            out_specs=pl.BlockSpec((n, size), lambda i, s: (0, 0)),
        ),
        out_shape=jax.ShapeDtypeStruct((n, size), F32),
        compiler_params=params(8),
        cost_estimate=cost(1, 8 * n * size),
        name="own_piece",
    )(at, far_memory(x))


def couple_kernel(at_ref, pin_ref, mine_ref, other_ref, out_ref):
    width = mine_ref.shape[1]
    side = at_ref[0] & 1
    out_ref[:, pl.ds(pl.multiple_of(side * width, width), width)] = mine_ref[...]
    out_ref[:, pl.ds(pl.multiple_of((1 - side) * width, width), width)] = other_ref[...]


def couple(at, pin, mine, other):
    n, width = mine.shape
    return pl.pallas_call(
        couple_kernel,
        in_specs=[SMALL, ANY, NEAR, NEAR],
        out_specs=NEAR,
        out_shape=jax.ShapeDtypeStruct((n, 2 * width), F32),
        compiler_params=params(4),
        cost_estimate=cost(1, 16 * n * width),
        name="couple",
    )(at, pin, mine, other)


def old_block(c, me, rows, width, pin):
    return pl.pallas_call(
        slice_kernel,
        grid_spec=pltpu.PrefetchScalarGridSpec(
            num_scalar_prefetch=1,
            grid=(2,),
            in_specs=[
                ANY,
                pl.BlockSpec((rows, width), lambda b, s: ((s[0] & 7) + 8 * b, s[0] // 8)),
            ],
            out_specs=pl.BlockSpec((rows, width), lambda b, s: (b, 0)),
        ),
        out_shape=jax.ShapeDtypeStruct((2 * rows, width), F32),
        compiler_params=params(4),
        cost_estimate=cost(1, 16 * rows * width),
        name="old_block",
    )(me, pin, far_memory(c))


def spread(me, sides, ch, cl):
    total = jnp.zeros((1, ch.shape[1]), F32)
    for side, ref in sides:
        rows = ref.shape[0] // 8

        def body(j, total):
            v = ref[pl.ds(pl.multiple_of(j * rows, rows), rows), :]
            hi, lo = split(v)
            at = (((me ^ (j // 2 * 2) ^ side) & 7) + 8 * (j % 2)) * rows
            at = pl.ds(pl.multiple_of(at, rows), rows)
            ch[at, :] = hi
            cl[at, :] = lo
            return total + jnp.sum(v * v, axis=0, keepdims=True)

        total = lax.fori_loop(0, 8, body, total)
    return 0.5 * total


def own_kernel(me_ref, mine_ref, other_ref, xh, xl, e_ref, stat_ref, ch, cl, norm, raw0, raw1):
    me = me_ref[0]
    half_norm = spread(
        me, ((0, mine_ref), (CORE, other_ref)), ch, cl
    )
    norm[...] = jnp.broadcast_to(half_norm, norm.shape)
    tile = raw0.shape[0]

    def finish(i, raw):
        at = pl.ds(pl.multiple_of(i * tile, tile), tile)
        for j, v in enumerate(softmax_part(raw, half_norm, e_ref, at)):
            stat_ref[j : j + 1, at] = v

    product = lambda i: dot3(
        xh[pl.ds(pl.multiple_of(i * tile, tile), tile), :], xl[pl.ds(pl.multiple_of(i * tile, tile), tile), :], ch[...], cl[...]
    )
    tiled(xh.shape[0] // tile, product, finish, (raw0, raw1))


def own_logits(me, mine, other, near, tile=256):
    n, d = near[0].shape
    k = mine.shape[1]
    return pl.pallas_call(
        own_kernel,
        in_specs=[SMALL] + [NEAR] * 4,
        out_specs=[NEAR] * 5,
        out_shape=[
            pltpu.VMEM((n, k), F32),
            jax.ShapeDtypeStruct((2, n), F32),
            pltpu.VMEM((d, k), BF16),
            pltpu.VMEM((d, k), BF16),
            pltpu.VMEM((8, k), F32),
        ],
        scratch_shapes=[pltpu.VMEM((tile, k), F32)] * 2,
        compiler_params=params(20),
        cost_estimate=cost(6 * n * d * k, 4 * (n * d + d * k + n * k)),
        name="own_logits",
    )(me, mine, other, *near)


def far_logits_kernel(me_ref, ch, cl, norm, own_ref, xh, xl, e_ref, stat_ref, raw0, raw1):
    tile = raw0.shape[0]
    n = own_ref.shape[1]
    z = me_ref[0] // 8
    stat_ref[:, pl.ds(pl.multiple_of(z * n, n), n)] = own_ref[...]

    def finish(i, raw):
        at = pl.ds(pl.multiple_of((1 - z) * n + i * tile, tile), tile)
        stats = softmax_part(raw, norm[0:1, :], e_ref, pl.ds(pl.multiple_of(i * tile, tile), tile))
        for j, v in enumerate(stats):
            stat_ref[j : j + 1, at] = v

    product = lambda i: dot3(
        xh[pl.ds(pl.multiple_of(i * tile, tile), tile), :], xl[pl.ds(pl.multiple_of(i * tile, tile), tile), :], ch[...], cl[...]
    )
    tiled(n // tile, product, finish, (raw0, raw1))


def far_logits(me, ch, cl, norm, own, far, tile=256):
    n, d = far[0].shape
    k = ch.shape[1]
    return pl.pallas_call(
        far_logits_kernel,
        in_specs=[SMALL] + [NEAR] * 6,
        out_specs=[NEAR] * 2,
        out_shape=[pltpu.VMEM((n, k), F32), jax.ShapeDtypeStruct((2, 2 * n), F32)],
        scratch_shapes=[pltpu.VMEM((tile, k), F32)] * 2,
        compiler_params=params(16),
        cost_estimate=cost(6 * n * d * k, 4 * (n * d + d * k + n * k)),
        name="far_logits",
    )(me, ch, cl, norm, own, *far)


def merge_kernel(pin_ref, mine_ref, other_ref, out_ref):
    top = jnp.maximum(mine_ref[0:1, :], other_ref[0:1, :])
    total = sum(ref[1:2, :] * jnp.exp(ref[0:1, :] - top) for ref in (mine_ref, other_ref))
    for i, v in enumerate((top, total)):
        out_ref[:, i : i + 1, :] = jnp.broadcast_to(v[None], (out_ref.shape[0], *v.shape))


def merge(pin, mine, other, copies):
    return pl.pallas_call(
        merge_kernel,
        in_specs=[ANY, NEAR, NEAR],
        out_specs=NEAR,
        out_shape=jax.ShapeDtypeStruct((copies, *mine.shape), F32),
        compiler_params=params(4),
        cost_estimate=cost(copies * mine.size, 8 * copies * mine.size),
        name="merge",
    )(pin, mine, other)


def row_scale(own, everyone):
    tops = everyone[:, 0, :]
    top = jnp.max(tops, axis=0, keepdims=True)
    total = jnp.sum(everyone[:, 1, :] * jnp.exp(tops - top), axis=0, keepdims=True)
    scale = jnp.exp(own[0:1, :] - top) / total
    return jnp.broadcast_to(scale, (128, scale.shape[1])).T[:, 0:1]


def permuted(order, low, ref, out):
    rows = ref.shape[0] // (2 * len(order))
    for j, r in enumerate(order):
        for b in range(2):
            at = pl.ds(pl.multiple_of(((low ^ r) + 8 * b) * rows, rows), rows)
            out[(2 * j + b) * rows : (2 * j + b + 1) * rows, :] = ref[at, :]


def emit(m, w, keep_ref, send_ref, at):
    half = m.shape[0] // 2
    mass = jnp.broadcast_to(jnp.sum(w, axis=0, keepdims=True), (PAD, w.shape[1]))
    keep_ref[0:half, at] = m[:half]
    send_ref[0:half, at] = m[half:]
    keep_ref[half : half + PAD, at] = mass
    send_ref[half : half + PAD, at] = mass


def first_moment_kernel(
    order, color, me_ref, pin_ref, own_ref, all_ref, th_ref, tl_ref, e_ref, keep_ref, send_ref, ph, pt
):
    low, z = me_ref[0] & 7, me_ref[0] // 8
    permuted(order, low, th_ref, ph)
    permuted(order, low, tl_ref, pt)
    scale = row_scale(own_ref[...], all_ref[...])
    width = e_ref.shape[1] // 4
    for h in range(2):
        column = pl.multiple_of((2 * (z ^ h) + color) * width, width)
        w = e_ref[:, pl.ds(column, width)] * scale
        wh, wl = split(w)
        m = dot3(ph[...], pt[...], wh, wl)
        emit(m, w, keep_ref, send_ref, slice(h * width, (h + 1) * width))


def first_moments(me, pin, own, everyone, th, tl, e, color, order):
    d, n = th.shape
    width = e.shape[1] // 4
    shape = jax.ShapeDtypeStruct((d // 2 + PAD, 2 * width), F32)
    return pl.pallas_call(
        functools.partial(first_moment_kernel, order, color),
        in_specs=[SMALL, ANY] + [NEAR] * 5,
        out_specs=[NEAR, NEAR],
        out_shape=[shape, shape],
        scratch_shapes=[pltpu.VMEM((d, n), BF16), pltpu.VMEM((d, n), BF16)],
        compiler_params=params(20),
        cost_estimate=cost(12 * d * n * width, 4 * (d * n + 2 * n * width + 2 * d * width)),
        name="first_moments",
    )(me, pin, own, everyone, th, tl, e)


def next_moment_kernel(
    order, color, me_ref, pin_ref, own, everyone, oh, ol, gh, gl, e0, e1, keep_ref, send_ref, ph, pt
):
    low, z = me_ref[0] & 7, me_ref[0] // 8
    n = e0.shape[0]
    width = e0.shape[1] // 2
    m = w_all = None
    for h, (th, tl, e) in enumerate(((oh, ol, e0), (gh, gl, e1))):
        at = pl.ds(pl.multiple_of((z ^ h) * n, n), n)
        permuted(order, low, th, ph)
        permuted(order, low, tl, pt)
        w = e[:, color * width : (color + 1) * width] * row_scale(own[:, at], everyone[:, :, at])
        wh, wl = split(w)
        part = dot3(ph[...], pt[...], wh, wl)
        m, w_all = (part, w) if m is None else (m + part, w_all + w)
    emit(m, w_all, keep_ref, send_ref, slice(None))


def next_moments(me, pin, own, everyone, near, far, e_own, e_far, color, order):
    d, n = near[0].shape
    width = e_own.shape[1] // 2
    shape = jax.ShapeDtypeStruct((d // 2 + PAD, width), F32)
    return pl.pallas_call(
        functools.partial(next_moment_kernel, order, color),
        in_specs=[SMALL, ANY] + [NEAR] * 8,
        out_specs=[NEAR, NEAR],
        out_shape=[shape, shape],
        scratch_shapes=[pltpu.VMEM((d, n), BF16)] * 2,
        compiler_params=params(20),
        cost_estimate=cost(12 * d * n * width, 4 * (2 * d * n + 2 * n * width + d * width)),
        name="next_moments",
    )(me, pin, own, everyone, *near, *far, e_own, e_far)


def relay_kernel(pin_ref, in_ref, out_ref):
    pass


def relay(a, pin):
    return pl.pallas_call(
        relay_kernel,
        in_specs=[ANY, ANY],
        out_specs=ANY,
        out_shape=jax.ShapeDtypeStruct(a.shape, a.dtype),
        input_output_aliases={1: 0},
        compiler_params=params(4),
        cost_estimate=cost(1, 1),
        name="relay",
    )(pin, a)


def chain(kernel, name, ins, shapes, pins=()):
    size = sum(a.size for a in ins)
    return pl.pallas_call(
        kernel,
        in_specs=[ANY] * len(pins) + [NEAR] * len(ins),
        out_shape=[jax.ShapeDtypeStruct(shape, F32) for shape in shapes],
        compiler_params=params(16),
        cost_estimate=cost(size, 8 * size),
        name=name,
    )(*pins, *ins)


def fold_kernel(pins, *refs):
    refs = refs[pins:]
    count = len(refs) // 4
    for u in range(count):
        keep, recv = refs[2 * u : 2 * u + 2]
        out, send = refs[2 * (count + u) : 2 * (count + u) + 2]
        half = (keep.shape[0] - PAD) // 2
        out[0:half, :] = keep[0:half, :] + recv[0:half, :]
        send[0:half, :] = keep[half : 2 * half, :] + recv[half : 2 * half, :]
        mass = keep[2 * half :, :] + recv[2 * half :, :]
        out[half:, :] = mass
        send[half:, :] = mass


def fold(ins, *pins):
    shapes = []
    for keep, _ in ins:
        shapes += [((keep.shape[0] - PAD) // 2 + PAD, keep.shape[1])] * 2
    kernel = functools.partial(fold_kernel, len(pins))
    flat = chain(kernel, "fold", [a for pair in ins for a in pair], shapes, pins)
    return [(flat[2 * i], flat[2 * i + 1]) for i in range(len(ins))]


def part_kernel(*refs):
    ins, (out, send) = refs[:-2], refs[-2:]
    for u in range(len(ins) // 2):
        keep, recv = ins[2 * u : 2 * u + 2]
        half = keep.shape[1] // 2
        cols = slice(u * half, (u + 1) * half)
        out[:, cols] = keep[:, 0:half] + recv[:, 0:half]
        send[:, cols] = keep[:, half:] + recv[:, half:]


def part(ins):
    rows, width = ins[0][0].shape
    shape = (rows, width // 2 * len(ins))
    return chain(part_kernel, "part", [a for pair in ins for a in pair], [shape] * 2)


def update_kernel(pins, *refs):
    keep, recv, old, out = refs[pins:]
    rows = old.shape[0]
    mass = keep[rows : rows + 1, :] + recv[rows : rows + 1, :] + 1.0
    out[...] = (keep[0:rows, :] + recv[0:rows, :] + old[...]) / mass


def update(keep, recv, old, *pins):
    kernel = functools.partial(update_kernel, len(pins))
    return chain(kernel, "update", [keep, recv, old], [old.shape], pins)[0]


def column_kernel(pins, *refs):
    refs = refs[pins:]
    rows = refs[0].shape[0]
    for i, ref in enumerate(refs[:-1]):
        refs[-1][i * rows : (i + 1) * rows, :] = ref[...]


def column(pieces, *pins):
    rows, width = pieces[0].shape
    kernel = functools.partial(column_kernel, len(pins))
    return chain(kernel, "column", pieces, [(rows * len(pieces), width)], pins)[0]


def last_kernel(me_ref, old, *refs):
    ins, (mine_ref, theirs_ref) = refs[:-2], refs[-2:]
    z = me_ref[0] // 8
    rows = old.shape[0]
    for u in range(len(ins) // 2):
        keep, recv = ins[2 * u : 2 * u + 2]
        cols = slice(u * keep.shape[1], (u + 1) * keep.shape[1])
        mass = keep[rows : rows + 1, :] + recv[rows : rows + 1, :] + 1.0
        for out, which in ((mine_ref, z), (theirs_ref, 1 - z)):
            at = pl.ds(pl.multiple_of(which * (rows // 2), rows // 2), rows // 2)
            out[:, cols] = (keep[at, :] + recv[at, :] + old[at, cols]) / mass


def last_update(me, ins, old):
    rows, width = old.shape
    shape = jax.ShapeDtypeStruct((rows // 2, width), F32)
    flat = [a for pair in ins for a in pair]
    return pl.pallas_call(
        last_kernel,
        in_specs=[SMALL] + [NEAR] * (1 + len(flat)),
        out_specs=[NEAR] * 2,
        out_shape=[shape, shape],
        compiler_params=params(16),
        cost_estimate=cost(8 * rows * width, 32 * rows * width),
        name="last_update",
    )(me, old, *flat)


def weights_kernel(
    me_ref,
    own_ref,
    all_ref,
    e_ref,
    xh_ref,
    xl_ref,
    mine_ref,
    other_ref,
    out_ref,
    tick_ref,
    ch,
    cl,
    norm,
):
    me = me_ref[0]
    z = me // 8

    @pl.when(pl.program_id(0) == 0)
    def _():
        sides = (0, mine_ref), (CORE, other_ref)
        norm[...] = jnp.broadcast_to(spread(me, sides, ch, cl), norm.shape)

    tops = all_ref[:, 0, :]
    top = jnp.max(tops, axis=0, keepdims=True)
    total = jnp.sum(all_ref[:, 1, :] * jnp.exp(tops - top), axis=0, keepdims=True)
    width = e_ref.shape[1]
    column = lambda v: jnp.broadcast_to(v, (128, v.shape[1])).T[:, 0:1]
    here = pl.ds(pl.multiple_of(z * width, width), width)
    there = pl.ds(pl.multiple_of((1 - z) * width, width), width)
    out_ref[:, here] = e_ref[...] * column(jnp.exp(own_ref[0:1, :] - top) / total)
    raw = dot3(xh_ref[...], xl_ref[...], ch[...], cl[...])
    logits = (raw - norm[0:1, :]) * 10.0
    out_ref[:, there] = jnp.exp(logits - column(top)) * column(1.0 / total)
    tick_ref[...] = norm[:, 0:128]


def final_weights(me, own, everyone, e_own, near, mine, other, tile=256):
    n, width = e_own.shape
    d = near[0].shape[1]
    t = n // tile
    rows = pl.BlockSpec((tile, d), lambda i, s: (i, 0))
    return pl.pallas_call(
        weights_kernel,
        grid_spec=pltpu.PrefetchScalarGridSpec(
            num_scalar_prefetch=1,
            grid=(t,),
            in_specs=[
                pl.BlockSpec((2, tile), lambda i, s: (0, (s[0] // 8) * t + i)),
                pl.BlockSpec(
                    (everyone.shape[0], 2, tile), lambda i, s: (0, 0, (s[0] // 8) * t + i)
                ),
                pl.BlockSpec((tile, width), lambda i, s: (i, 0)),
                rows,
                rows,
                NEAR,
                NEAR,
            ],
            out_specs=[pl.BlockSpec((tile, 2 * width), lambda i, s: (i, 0)), NEAR],
            scratch_shapes=[
                pltpu.VMEM((d, width), BF16),
                pltpu.VMEM((d, width), BF16),
                pltpu.VMEM((8, width), F32),
            ],
        ),
        out_shape=[pltpu.HBM((n, 2 * width), F32), jax.ShapeDtypeStruct((8, 128), F32)],
        compiler_params=params(24),
        cost_estimate=cost(6 * n * width * d, 4 * (n * d + 3 * n * width + d * width)),
        name="weights",
    )(me, own, everyone, e_own, *near, mine, other)


def local(x, c):
    index = lax.axis_index("pts").astype(jnp.int32)
    me = index.reshape(1)
    place_cen = lax.axis_index("cen").astype(jnp.int32)
    run, y = place_cen & 3, place_cen // 4
    at = jnp.stack([y * 2 + (run & 1), run >> 1, run, y])
    d, k = c.shape
    rows = d // 16
    cen = lax.axis_size("cen")
    along_y = lambda v, shift: lax.ppermute(
        v, "cen", [(j, (j + 4 * shift) % cen) for j in range(cen)]
    )

    piece = own_piece(x, at)
    e, stats, copies, xh, xl, th, tl = first_step(me, at, piece, x, c, cen)
    piece = swap(piece, ZG)
    everyone = lax.all_to_all(copies, "cen", 0, 0)
    orders = [relative_blocks(gens) for gens in COLORS]
    swapped = lambda units, step: [
        (keep, swap(send, gens[step])) for gens, (keep, send) in zip(COLORS, units)
    ]
    units, pin = [], piece
    for u, order in enumerate(orders):
        units.append(first_moments(me, pin, stats, everyone, th, tl, e, u, order))
        pin = units[-1][1]
    old = old_block(c, me, rows, k // 2, pin)
    other = lax.ppermute(relay(piece, units[0][1]), "cen", [(j, j ^ 1) for j in range(cen)])
    quarter = couple(at, old, piece, other)
    units = fold(swapped(units, 0))
    units = fold(swapped(units, 1), quarter)
    quarters = [quarter] + [along_y(quarter, shift) for shift in (1, 2, 3)]
    keep, send = part(swapped(units, 2))
    share = update(keep, swap(send, ZG), old)
    joint = swap(share, ZG)
    mine = column([share] + [swap(share, mask) for mask in X_PEERS], *quarters[1:])
    fh, fl, gh, gl = far_points(at, quarters)
    e_own, stats, ch, cl, norm = own_logits(me, mine, swap(mine, CORE), (xh, xl))
    e_far, stats = far_logits(me, ch, cl, norm, stats, (fh, fl))
    everyone = lax.all_to_all(merge(joint, stats, swap(stats, ZG), cen), "cen", 0, 0)
    joint = relay(joint, everyone)
    peers = [joint] + [swap(joint, mask) for mask in X_PEERS]
    units, pin = [], everyone
    for u, order in enumerate(orders):
        units.append(
            next_moments(me, pin, stats, everyone, (th, tl), (gh, gl), e_own, e_far, u, order)
        )
        pin = units[-1][1]
    far_mine = column(peers, pin)
    units = fold(swapped(units, 0))
    units = fold(swapped(units, 1))
    far_other = swap(far_mine, CORE)
    weights, tick = final_weights(me, stats, everyone, e_own, (xh, xl), far_mine, far_other)
    mine, theirs = last_update(me, swapped(units, 2), share)
    return weights, place(me, tick, mine, swap(theirs, ZG))


def place_kernel(me_ref, pin_ref, mine_ref, other_ref, out_ref):
    z = me_ref[0] // 8
    width = mine_ref.shape[1]
    out_ref[:, pl.ds(pl.multiple_of(z * width, width), width)] = mine_ref[...]
    out_ref[:, pl.ds(pl.multiple_of((1 - z) * width, width), width)] = other_ref[...]


def place(me, pin, mine, other):
    rows, width = mine.shape
    return pl.pallas_call(
        place_kernel,
        in_specs=[SMALL, ANY, NEAR, NEAR],
        out_specs=NEAR,
        out_shape=jax.ShapeDtypeStruct((rows, 2 * width), F32),
        compiler_params=params(4),
        cost_estimate=cost(1, 16 * rows * width),
        name="place",
    )(me, pin, mine, other)


def solution(mesh):
    placed = (P("pts", None), P(None, "cen"))
    return jax.shard_map(
        local,
        mesh=mesh,
        in_specs=placed,
        out_specs=(P("pts", "cen"), P("pts", "cen")),
        check_vma=False,
    )
```

```python
import functools

import jax
import jax.numpy as jnp
from jax import lax
from jax.experimental import pallas as pl
from jax.experimental.pallas import tpu as pltpu
from jax.sharding import PartitionSpec as P

F32 = jnp.float32
BF16 = jnp.bfloat16
PAD = 8
MIB = 1 << 20
CORE, XA, XB, ZG = 1, 2, 6, 8
X_PEERS = (2, 4, 6)
COLORS = ((CORE, XA, XB), (CORE, XB, XA))
COST = 0.1


def split(v):
    hi = v.astype(BF16)
    return hi, (v - hi.astype(F32)).astype(BF16)


def dot3(ah, al, bh, bl):
    dot = functools.partial(jnp.dot, preferred_element_type=F32)
    return dot(ah, bh) + (dot(ah, bl) + dot(al, bh))


def swap(v, g):
    return lax.ppermute(v, "pts", [(i, i ^ g) for i in range(lax.axis_size("pts"))])


def relative_blocks(gens):
    out = [0]
    for g in reversed(gens):
        out = out + [r ^ g for r in out]
    return out


def params(mib):
    return pltpu.CompilerParams(vmem_limit_bytes=mib * MIB)


def cost(flops, nbytes):
    return pl.CostEstimate(
        flops=int(flops * COST), bytes_accessed=int(nbytes * COST), transcendentals=0
    )


def far_memory(*arrays):
    out = [pltpu.with_memory_space_constraint(a, pltpu.HBM) for a in arrays]
    return out[0] if len(out) == 1 else out


def near_memory(*arrays):
    return [pltpu.with_memory_space_constraint(a, pltpu.VMEM) for a in arrays]


ANY = pl.BlockSpec(memory_space=pl.ANY)
SMALL = pl.BlockSpec(memory_space=pltpu.SMEM)
NEAR = pl.BlockSpec(memory_space=pltpu.VMEM)


def whole(a):
    return pl.BlockSpec(a.shape, lambda i, s: (0,) * len(a.shape))


def softmax_part(raw_ref, half_norm, e_ref, at):
    logits = (raw_ref[...] - half_norm) * 10.0
    top = jnp.max(logits, axis=1, keepdims=True)
    expo = jnp.exp(logits - top)
    total = jnp.sum(expo, axis=1, keepdims=True)
    e_ref[at, :] = expo
    row = lambda v: jnp.broadcast_to(v, (v.shape[0], 128)).T[0:1, :]
    return row(top), row(total)


def tiled3(tiles, product, finish, raws):
    for i in range(tiles + 1):
        if i < tiles:
            raws[i % 2][...] = product(i)
        if i > 0:
            finish(i - 1, raws[(i - 1) % 2])


def tiled(tiles, product, finish, raws):
    @pl.loop(0, tiles)
    def _(i):
        raws[0][...] = product(i)
        finish(i, raws[0])


def put_stats(stats, stat_ref, all_ref, at):
    for i, v in enumerate(stats):
        stat_ref[i : i + 1, at] = v
        all_ref[:, i : i + 1, at] = jnp.broadcast_to(v[None], (all_ref.shape[0], *v.shape))


def first_kernel(
    me_ref,
    at_ref,
    pin_ref,
    x_ref,
    c_ref,
    e_ref,
    stat_ref,
    all_ref,
    xh_ref,
    xl_ref,
    th_ref,
    tl_ref,
    xs,
    cs,
    ch,
    cl,
    raw0,
    raw1,
    sems,
):
    tile = raw0.shape[0]
    tiles = x_ref.shape[0] // tile
    chunks = sems.shape[0] - tiles
    step = c_ref.shape[0] // chunks
    c_at = [pl.ds(j * step, step) for j in range(chunks)]
    x_at = [pl.ds(j * tile, tile) for j in range(tiles)]
    c_in = [
        pltpu.make_async_copy(c_ref.at[at, :], cs.at[at, :], sems.at[j])
        for j, at in enumerate(c_at)
    ]
    x_in = [
        pltpu.make_async_copy(x_ref.at[at, :], xs.at[at, :], sems.at[chunks + j])
        for j, at in enumerate(x_at)
    ]
    for copy in c_in + x_in:
        copy.start()
    total = jnp.zeros((1, cs.shape[1]), F32)
    def arrived(j, total):
        at = pl.ds(pl.multiple_of(j * step, step), step)
        pltpu.make_async_copy(c_ref.at[at, :], cs.at[at, :], sems.at[j]).wait()
        v = cs[at, :]
        ch[at, :], cl[at, :] = split(v)
        return total + jnp.sum(v * v, axis=0, keepdims=True)

    total = lax.fori_loop(0, chunks, arrived, total)
    half_norm = 0.5 * total

    def product(i):
        at = x_at[i]
        x_in[i].wait()
        x = xs[at, :]
        hi, lo = split(x)
        xh_ref[at, :] = hi
        xl_ref[at, :] = lo
        th_ref[:, at], tl_ref[:, at] = split(x.T)
        return dot3(hi, lo, ch[...], cl[...])

    def finish(i, raw):
        put_stats(softmax_part(raw, half_norm, e_ref, x_at[i]), stat_ref, all_ref, x_at[i])

    tiled3(tiles, product, finish, (raw0, raw1))


def first_step(me, at, pin, x, c, copies, tile=256, chunks=8):
    n, d = x.shape
    k = c.shape[1]
    return pl.pallas_call(
        first_kernel,
        in_specs=[SMALL, SMALL, ANY, ANY, ANY],
        out_specs=[NEAR] * 7,
        out_shape=[
            pltpu.VMEM((n, k), F32),
            jax.ShapeDtypeStruct((2, n), F32),
            jax.ShapeDtypeStruct((copies, 2, n), F32),
            pltpu.VMEM((n, d), BF16),
            pltpu.VMEM((n, d), BF16),
            pltpu.VMEM((d, n), BF16),
            pltpu.VMEM((d, n), BF16),
        ],
        scratch_shapes=[
            pltpu.VMEM((n, d), F32),
            pltpu.VMEM((d, k), F32),
            pltpu.VMEM((d, k), BF16),
            pltpu.VMEM((d, k), BF16),
            pltpu.VMEM((tile, k), F32),
            pltpu.VMEM((tile, k), F32),
            pltpu.SemaphoreType.DMA((chunks + n // tile,)),
        ],
        compiler_params=params(36),
        cost_estimate=cost(20 * 6 * n * d * k, 4 * (2 * n * d + d * k + n * k)),
        name="first_logits",
    )(me, at, pin, *far_memory(x, c))


def far_kernel(at_ref, *refs):
    pieces, (xh_ref, xl_ref, th_ref, tl_ref) = refs[:4], refs[4:]
    width = pieces[0].shape[1]
    for shift, piece in enumerate(pieces):
        quarter = lax.rem(at_ref[3] - shift + 4, 4)
        at = pl.ds(pl.multiple_of(quarter * width, width), width)
        v = piece[...]
        xh_ref[:, at], xl_ref[:, at] = split(v)
        th_ref[at, :], tl_ref[at, :] = split(v.T)


def far_points(at, pieces):
    n, width = pieces[0].shape
    d = width * len(pieces)
    return pl.pallas_call(
        far_kernel,
        in_specs=[SMALL] + [NEAR] * len(pieces),
        out_specs=[NEAR] * 4,
        out_shape=[pltpu.VMEM(s, BF16) for s in ((n, d), (n, d), (d, n), (d, n))],
        compiler_params=params(16),
        cost_estimate=cost(4 * n * d, 12 * n * d),
        name="far_points",
    )(at, *pieces)


def slice_kernel(at_ref, pin_ref, x_ref, out_ref):
    out_ref[...] = x_ref[...]


def own_piece(x, at):
    n, size = x.shape[0], x.shape[1] // 8
    return pl.pallas_call(
        lambda at_ref, x_ref, out_ref: slice_kernel(at_ref, None, x_ref, out_ref),
        grid_spec=pltpu.PrefetchScalarGridSpec(
            num_scalar_prefetch=1,
            grid=(1,),
            in_specs=[pl.BlockSpec((n, size), lambda i, s: (0, s[0]))],
            out_specs=pl.BlockSpec((n, size), lambda i, s: (0, 0)),
        ),
        out_shape=jax.ShapeDtypeStruct((n, size), F32),
        compiler_params=params(8),
        cost_estimate=cost(1, 8 * n * size),
        name="own_piece",
    )(at, far_memory(x))


def couple_kernel(at_ref, pin_ref, mine_ref, other_ref, out_ref):
    width = mine_ref.shape[1]
    side = at_ref[0] & 1
    out_ref[:, pl.ds(pl.multiple_of(side * width, width), width)] = mine_ref[...]
    out_ref[:, pl.ds(pl.multiple_of((1 - side) * width, width), width)] = other_ref[...]


def couple(at, pin, mine, other):
    n, width = mine.shape
    return pl.pallas_call(
        couple_kernel,
        in_specs=[SMALL, ANY, NEAR, NEAR],
        out_specs=NEAR,
        out_shape=jax.ShapeDtypeStruct((n, 2 * width), F32),
        compiler_params=params(4),
        cost_estimate=cost(1, 16 * n * width),
        name="couple",
    )(at, pin, mine, other)


def old_block(c, me, rows, width, pin):
    return pl.pallas_call(
        slice_kernel,
        grid_spec=pltpu.PrefetchScalarGridSpec(
            num_scalar_prefetch=1,
            grid=(2,),
            in_specs=[
                ANY,
                pl.BlockSpec((rows, width), lambda b, s: ((s[0] & 7) + 8 * b, s[0] // 8)),
            ],
            out_specs=pl.BlockSpec((rows, width), lambda b, s: (b, 0)),
        ),
        out_shape=jax.ShapeDtypeStruct((2 * rows, width), F32),
        compiler_params=params(4),
        cost_estimate=cost(1, 16 * rows * width),
        name="old_block",
    )(me, pin, far_memory(c))


def spread(me, sides, ch, cl):
    total = jnp.zeros((1, ch.shape[1]), F32)
    for side, ref in sides:
        rows = ref.shape[0] // 8

        def body(j, total):
            v = ref[pl.ds(pl.multiple_of(j * rows, rows), rows), :]
            hi, lo = split(v)
            at = (((me ^ (j // 2 * 2) ^ side) & 7) + 8 * (j % 2)) * rows
            at = pl.ds(pl.multiple_of(at, rows), rows)
            ch[at, :] = hi
            cl[at, :] = lo
            return total + jnp.sum(v * v, axis=0, keepdims=True)

        total = lax.fori_loop(0, 8, body, total)
    return 0.5 * total


def own_kernel(me_ref, mine_ref, other_ref, xh, xl, e_ref, stat_ref, ch, cl, norm, raw0, raw1):
    me = me_ref[0]
    half_norm = spread(
        me, ((0, mine_ref), (CORE, other_ref)), ch, cl
    )
    norm[...] = jnp.broadcast_to(half_norm, norm.shape)
    tile = raw0.shape[0]

    def finish(i, raw):
        at = pl.ds(pl.multiple_of(i * tile, tile), tile)
        for j, v in enumerate(softmax_part(raw, half_norm, e_ref, at)):
            stat_ref[j : j + 1, at] = v

    product = lambda i: dot3(
        xh[pl.ds(pl.multiple_of(i * tile, tile), tile), :], xl[pl.ds(pl.multiple_of(i * tile, tile), tile), :], ch[...], cl[...]
    )
    tiled(xh.shape[0] // tile, product, finish, (raw0, raw1))


def own_logits(me, mine, other, near, tile=256):
    n, d = near[0].shape
    k = mine.shape[1]
    return pl.pallas_call(
        own_kernel,
        in_specs=[SMALL] + [NEAR] * 4,
        out_specs=[NEAR] * 5,
        out_shape=[
            pltpu.VMEM((n, k), F32),
            jax.ShapeDtypeStruct((2, n), F32),
            pltpu.VMEM((d, k), BF16),
            pltpu.VMEM((d, k), BF16),
            pltpu.VMEM((8, k), F32),
        ],
        scratch_shapes=[pltpu.VMEM((tile, k), F32)] * 2,
        compiler_params=params(20),
        cost_estimate=cost(6 * n * d * k, 4 * (n * d + d * k + n * k)),
        name="own_logits",
    )(me, mine, other, *near)


def far_logits_kernel(me_ref, ch, cl, norm, own_ref, xh, xl, e_ref, stat_ref, raw0, raw1):
    tile = raw0.shape[0]
    n = own_ref.shape[1]
    z = me_ref[0] // 8
    stat_ref[:, pl.ds(pl.multiple_of(z * n, n), n)] = own_ref[...]

    def finish(i, raw):
        at = pl.ds(pl.multiple_of((1 - z) * n + i * tile, tile), tile)
        stats = softmax_part(raw, norm[0:1, :], e_ref, pl.ds(pl.multiple_of(i * tile, tile), tile))
        for j, v in enumerate(stats):
            stat_ref[j : j + 1, at] = v

    product = lambda i: dot3(
        xh[pl.ds(pl.multiple_of(i * tile, tile), tile), :], xl[pl.ds(pl.multiple_of(i * tile, tile), tile), :], ch[...], cl[...]
    )
    tiled(n // tile, product, finish, (raw0, raw1))


def far_logits(me, ch, cl, norm, own, far, tile=256):
    n, d = far[0].shape
    k = ch.shape[1]
    return pl.pallas_call(
        far_logits_kernel,
        in_specs=[SMALL] + [NEAR] * 6,
        out_specs=[NEAR] * 2,
        out_shape=[pltpu.VMEM((n, k), F32), jax.ShapeDtypeStruct((2, 2 * n), F32)],
        scratch_shapes=[pltpu.VMEM((tile, k), F32)] * 2,
        compiler_params=params(16),
        cost_estimate=cost(6 * n * d * k, 4 * (n * d + d * k + n * k)),
        name="far_logits",
    )(me, ch, cl, norm, own, *far)


def merge_kernel(p1, p2, p3, mine_ref, other_ref, out_ref):
    top = jnp.maximum(mine_ref[0:1, :], other_ref[0:1, :])
    total = sum(ref[1:2, :] * jnp.exp(ref[0:1, :] - top) for ref in (mine_ref, other_ref))
    for i, v in enumerate((top, total)):
        out_ref[:, i : i + 1, :] = jnp.broadcast_to(v[None], (out_ref.shape[0], *v.shape))


def merge(pins, mine, other, copies):
    return pl.pallas_call(
        merge_kernel,
        in_specs=[ANY] * 3 + [NEAR, NEAR],
        out_specs=NEAR,
        out_shape=jax.ShapeDtypeStruct((copies, *mine.shape), F32),
        compiler_params=params(4),
        cost_estimate=cost(copies * mine.size, 8 * copies * mine.size),
        name="merge",
    )(*pins, mine, other)


def row_scale(own, everyone):
    tops = everyone[:, 0, :]
    top = jnp.max(tops, axis=0, keepdims=True)
    total = jnp.sum(everyone[:, 1, :] * jnp.exp(tops - top), axis=0, keepdims=True)
    scale = jnp.exp(own[0:1, :] - top) / total
    return jnp.broadcast_to(scale, (128, scale.shape[1])).T[:, 0:1]


def permuted(order, low, ref, out):
    rows = ref.shape[0] // (2 * len(order))
    for j, r in enumerate(order):
        for b in range(2):
            at = pl.ds(pl.multiple_of(((low ^ r) + 8 * b) * rows, rows), rows)
            out[(2 * j + b) * rows : (2 * j + b + 1) * rows, :] = ref[at, :]


def emit(m, w, keep_ref, send_ref, at):
    half = m.shape[0] // 2
    mass = jnp.broadcast_to(jnp.sum(w, axis=0, keepdims=True), (PAD, w.shape[1]))
    keep_ref[0:half, at] = m[:half]
    send_ref[0:half, at] = m[half:]
    keep_ref[half : half + PAD, at] = mass
    send_ref[half : half + PAD, at] = mass


def first_moment_kernel(
    order, color, me_ref, pin_ref, own_ref, all_ref, th_ref, tl_ref, e_ref, keep_ref, send_ref, ph, pt
):
    low, z = me_ref[0] & 7, me_ref[0] // 8
    permuted(order, low, th_ref, ph)
    permuted(order, low, tl_ref, pt)
    scale = row_scale(own_ref[...], all_ref[...])
    width = e_ref.shape[1] // 4
    for h in range(2):
        column = pl.multiple_of((2 * (z ^ h) + color) * width, width)
        w = e_ref[:, pl.ds(column, width)] * scale
        wh, wl = split(w)
        m = dot3(ph[...], pt[...], wh, wl)
        emit(m, w, keep_ref, send_ref, slice(h * width, (h + 1) * width))


def first_moments(me, pin, own, everyone, th, tl, e, color, order):
    d, n = th.shape
    width = e.shape[1] // 4
    shape = jax.ShapeDtypeStruct((d // 2 + PAD, 2 * width), F32)
    return pl.pallas_call(
        functools.partial(first_moment_kernel, order, color),
        in_specs=[SMALL, ANY] + [NEAR] * 5,
        out_specs=[NEAR, NEAR],
        out_shape=[shape, shape],
        scratch_shapes=[pltpu.VMEM((d, n), BF16), pltpu.VMEM((d, n), BF16)],
        compiler_params=params(20),
        cost_estimate=cost(12 * d * n * width, 4 * (d * n + 2 * n * width + 2 * d * width)),
        name="first_moments",
    )(me, pin, own, everyone, th, tl, e)


def next_moment_kernel(
    order, color, me_ref, pin_ref, own, everyone, oh, ol, gh, gl, e0, e1, keep_ref, send_ref, ph, pt
):
    low, z = me_ref[0] & 7, me_ref[0] // 8
    n = e0.shape[0]
    width = e0.shape[1] // 2
    m = w_all = None
    for h, (th, tl, e) in enumerate(((oh, ol, e0), (gh, gl, e1))):
        at = pl.ds(pl.multiple_of((z ^ h) * n, n), n)
        permuted(order, low, th, ph)
        permuted(order, low, tl, pt)
        w = e[:, color * width : (color + 1) * width] * row_scale(own[:, at], everyone[:, :, at])
        wh, wl = split(w)
        part = dot3(ph[...], pt[...], wh, wl)
        m, w_all = (part, w) if m is None else (m + part, w_all + w)
    emit(m, w_all, keep_ref, send_ref, slice(None))


def next_moments(me, pin, own, everyone, near, far, e_own, e_far, color, order):
    d, n = near[0].shape
    width = e_own.shape[1] // 2
    shape = jax.ShapeDtypeStruct((d // 2 + PAD, width), F32)
    return pl.pallas_call(
        functools.partial(next_moment_kernel, order, color),
        in_specs=[SMALL, ANY] + [NEAR] * 8,
        out_specs=[NEAR, NEAR],
        out_shape=[shape, shape],
        scratch_shapes=[pltpu.VMEM((d, n), BF16)] * 2,
        compiler_params=params(20),
        cost_estimate=cost(12 * d * n * width, 4 * (2 * d * n + 2 * n * width + d * width)),
        name="next_moments",
    )(me, pin, own, everyone, *near, *far, e_own, e_far)


def relay_kernel(pin_ref, in_ref, out_ref):
    pass


def relay(a, pin):
    return pl.pallas_call(
        relay_kernel,
        in_specs=[ANY, ANY],
        out_specs=ANY,
        out_shape=jax.ShapeDtypeStruct(a.shape, a.dtype),
        input_output_aliases={1: 0},
        compiler_params=params(4),
        cost_estimate=cost(1, 1),
        name="relay",
    )(pin, a)


def chain(kernel, name, ins, shapes, pins=()):
    size = sum(a.size for a in ins)
    return pl.pallas_call(
        kernel,
        in_specs=[ANY] * len(pins) + [NEAR] * len(ins),
        out_shape=[jax.ShapeDtypeStruct(shape, F32) for shape in shapes],
        compiler_params=params(16),
        cost_estimate=cost(size, 8 * size),
        name=name,
    )(*pins, *ins)


def fold_kernel(pins, *refs):
    refs = refs[pins:]
    count = len(refs) // 4
    for u in range(count):
        keep, recv = refs[2 * u : 2 * u + 2]
        out, send = refs[2 * (count + u) : 2 * (count + u) + 2]
        half = (keep.shape[0] - PAD) // 2
        out[0:half, :] = keep[0:half, :] + recv[0:half, :]
        send[0:half, :] = keep[half : 2 * half, :] + recv[half : 2 * half, :]
        mass = keep[2 * half :, :] + recv[2 * half :, :]
        out[half:, :] = mass
        send[half:, :] = mass


def fold(ins, *pins):
    shapes = []
    for keep, _ in ins:
        shapes += [((keep.shape[0] - PAD) // 2 + PAD, keep.shape[1])] * 2
    kernel = functools.partial(fold_kernel, len(pins))
    flat = chain(kernel, "fold", [a for pair in ins for a in pair], shapes, pins)
    return [(flat[2 * i], flat[2 * i + 1]) for i in range(len(ins))]


def part_kernel(*refs):
    ins, (out, send) = refs[:-2], refs[-2:]
    for u in range(len(ins) // 2):
        keep, recv = ins[2 * u : 2 * u + 2]
        half = keep.shape[1] // 2
        cols = slice(u * half, (u + 1) * half)
        out[:, cols] = keep[:, 0:half] + recv[:, 0:half]
        send[:, cols] = keep[:, half:] + recv[:, half:]


def part(ins):
    rows, width = ins[0][0].shape
    shape = (rows, width // 2 * len(ins))
    return chain(part_kernel, "part", [a for pair in ins for a in pair], [shape] * 2)


def update_kernel(pins, *refs):
    keep, recv, old, out = refs[pins:]
    rows = old.shape[0]
    mass = keep[rows : rows + 1, :] + recv[rows : rows + 1, :] + 1.0
    out[...] = (keep[0:rows, :] + recv[0:rows, :] + old[...]) / mass


def update(keep, recv, old, *pins):
    kernel = functools.partial(update_kernel, len(pins))
    return chain(kernel, "update", [keep, recv, old], [old.shape], pins)[0]


def column_kernel(pins, *refs):
    refs = refs[pins:]
    rows = refs[0].shape[0]
    for i, ref in enumerate(refs[:-1]):
        refs[-1][i * rows : (i + 1) * rows, :] = ref[...]


def column(pieces, *pins):
    rows, width = pieces[0].shape
    kernel = functools.partial(column_kernel, len(pins))
    return chain(kernel, "column", pieces, [(rows * len(pieces), width)], pins)[0]


def last_kernel(me_ref, old, *refs):
    ins, (mine_ref, theirs_ref) = refs[:-2], refs[-2:]
    z = me_ref[0] // 8
    rows = old.shape[0]
    for u in range(len(ins) // 2):
        keep, recv = ins[2 * u : 2 * u + 2]
        cols = slice(u * keep.shape[1], (u + 1) * keep.shape[1])
        mass = keep[rows : rows + 1, :] + recv[rows : rows + 1, :] + 1.0
        for out, which in ((mine_ref, z), (theirs_ref, 1 - z)):
            at = pl.ds(pl.multiple_of(which * (rows // 2), rows // 2), rows // 2)
            out[:, cols] = (keep[at, :] + recv[at, :] + old[at, cols]) / mass


def last_update(me, ins, old):
    rows, width = old.shape
    shape = jax.ShapeDtypeStruct((rows // 2, width), F32)
    flat = [a for pair in ins for a in pair]
    return pl.pallas_call(
        last_kernel,
        in_specs=[SMALL] + [NEAR] * (1 + len(flat)),
        out_specs=[NEAR] * 2,
        out_shape=[shape, shape],
        compiler_params=params(16),
        cost_estimate=cost(8 * rows * width, 32 * rows * width),
        name="last_update",
    )(me, old, *flat)


def weights_kernel(
    me_ref,
    own_ref,
    all_ref,
    e_ref,
    xh_ref,
    xl_ref,
    mine_ref,
    other_ref,
    out_ref,
    tick_ref,
    ch,
    cl,
    norm,
):
    me = me_ref[0]
    z = me // 8

    @pl.when(pl.program_id(0) == 0)
    def _():
        sides = (0, mine_ref), (CORE, other_ref)
        norm[...] = jnp.broadcast_to(spread(me, sides, ch, cl), norm.shape)

    tops = all_ref[:, 0, :]
    top = jnp.max(tops, axis=0, keepdims=True)
    total = jnp.sum(all_ref[:, 1, :] * jnp.exp(tops - top), axis=0, keepdims=True)
    width = e_ref.shape[1]
    column = lambda v: jnp.broadcast_to(v, (128, v.shape[1])).T[:, 0:1]
    here = pl.ds(pl.multiple_of(z * width, width), width)
    there = pl.ds(pl.multiple_of((1 - z) * width, width), width)
    out_ref[:, here] = e_ref[...] * column(jnp.exp(own_ref[0:1, :] - top) / total)
    raw = dot3(xh_ref[...], xl_ref[...], ch[...], cl[...])
    logits = (raw - norm[0:1, :]) * 10.0
    out_ref[:, there] = jnp.exp(logits - column(top)) * column(1.0 / total)
    tick_ref[...] = norm[:, 0:128]


def final_weights(me, own, everyone, e_own, near, mine, other, tile=256):
    n, width = e_own.shape
    d = near[0].shape[1]
    t = n // tile
    rows = pl.BlockSpec((tile, d), lambda i, s: (i, 0))
    return pl.pallas_call(
        weights_kernel,
        grid_spec=pltpu.PrefetchScalarGridSpec(
            num_scalar_prefetch=1,
            grid=(t,),
            in_specs=[
                pl.BlockSpec((2, tile), lambda i, s: (0, (s[0] // 8) * t + i)),
                pl.BlockSpec(
                    (everyone.shape[0], 2, tile), lambda i, s: (0, 0, (s[0] // 8) * t + i)
                ),
                pl.BlockSpec((tile, width), lambda i, s: (i, 0)),
                rows,
                rows,
                NEAR,
                NEAR,
            ],
            out_specs=[pl.BlockSpec((tile, 2 * width), lambda i, s: (i, 0)), NEAR],
            scratch_shapes=[
                pltpu.VMEM((d, width), BF16),
                pltpu.VMEM((d, width), BF16),
                pltpu.VMEM((8, width), F32),
            ],
        ),
        out_shape=[pltpu.HBM((n, 2 * width), F32), jax.ShapeDtypeStruct((8, 128), F32)],
        compiler_params=params(24),
        cost_estimate=cost(6 * n * width * d, 4 * (n * d + 3 * n * width + d * width)),
        name="weights",
    )(me, own, everyone, e_own, *near, mine, other)


def local(x, c):
    index = lax.axis_index("pts").astype(jnp.int32)
    me = index.reshape(1)
    place_cen = lax.axis_index("cen").astype(jnp.int32)
    run, y = place_cen & 3, place_cen // 4
    at = jnp.stack([y * 2 + (run & 1), run >> 1, run, y])
    d, k = c.shape
    rows = d // 16
    cen = lax.axis_size("cen")
    along_y = lambda v, shift: lax.ppermute(
        v, "cen", [(j, (j + 4 * shift) % cen) for j in range(cen)]
    )

    piece = own_piece(x, at)
    e, stats, copies, xh, xl, th, tl = first_step(me, at, piece, x, c, cen)
    piece = swap(piece, ZG)
    everyone = lax.all_to_all(copies, "cen", 0, 0)
    orders = [relative_blocks(gens) for gens in COLORS]
    swapped = lambda units, step: [
        (keep, swap(send, gens[step])) for gens, (keep, send) in zip(COLORS, units)
    ]
    units, pin = [], piece
    for u, order in enumerate(orders):
        units.append(first_moments(me, pin, stats, everyone, th, tl, e, u, order))
        pin = units[-1][1]
    old = old_block(c, me, rows, k // 2, pin)
    other = lax.ppermute(relay(piece, units[0][1]), "cen", [(j, j ^ 1) for j in range(cen)])
    quarter = couple(at, old, piece, other)
    units = fold(swapped(units, 0))
    units = fold(swapped(units, 1), quarter)
    quarters = [quarter] + [along_y(quarter, shift) for shift in (1, 2, 3)]
    keep, send = part(swapped(units, 2))
    share = update(keep, swap(send, ZG), old)
    joint = swap(share, ZG)
    mine = column([share] + [swap(share, mask) for mask in X_PEERS], *quarters[1:], joint)
    fh, fl, gh, gl = far_points(at, quarters)
    e_own, stats, ch, cl, norm = own_logits(me, mine, swap(mine, CORE), (xh, xl))
    peers = [joint] + [swap(joint, mask) for mask in X_PEERS]
    e_far, stats = far_logits(me, ch, cl, norm, stats, (fh, fl))
    everyone = lax.all_to_all(merge(peers[1:], stats, swap(stats, ZG), cen), "cen", 0, 0)
    units, pin = [], everyone
    for u, order in enumerate(orders):
        units.append(
            next_moments(me, pin, stats, everyone, (th, tl), (gh, gl), e_own, e_far, u, order)
        )
        pin = units[-1][1]
    far_mine = column(peers, pin)
    units = fold(swapped(units, 0))
    units = fold(swapped(units, 1))
    far_other = swap(far_mine, CORE)
    weights, tick = final_weights(me, stats, everyone, e_own, (xh, xl), far_mine, far_other)
    mine, theirs = last_update(me, swapped(units, 2), share)
    return weights, place(me, tick, mine, swap(theirs, ZG))


def place_kernel(me_ref, pin_ref, mine_ref, other_ref, out_ref):
    z = me_ref[0] // 8
    width = mine_ref.shape[1]
    out_ref[:, pl.ds(pl.multiple_of(z * width, width), width)] = mine_ref[...]
    out_ref[:, pl.ds(pl.multiple_of((1 - z) * width, width), width)] = other_ref[...]


def place(me, pin, mine, other):
    rows, width = mine.shape
    return pl.pallas_call(
        place_kernel,
        in_specs=[SMALL, ANY, NEAR, NEAR],
        out_specs=NEAR,
        out_shape=jax.ShapeDtypeStruct((rows, 2 * width), F32),
        compiler_params=params(4),
        cost_estimate=cost(1, 16 * rows * width),
        name="place",
    )(me, pin, mine, other)


def solution(mesh):
    placed = (P("pts", None), P(None, "cen"))
    return jax.shard_map(
        local,
        mesh=mesh,
        in_specs=placed,
        out_specs=(P("pts", "cen"), P("pts", "cen")),
        check_vma=False,
    )
```
